128 devices in a mesh: zg: 4 (over z_hi, core), xy: 32 (over z_lo, y, x).
Axes of the slice: x: 4, y: 4, z: 4 (z_hi: 2, z_lo: 2; z = z_hi * 2 + z_lo), core: 2. Of those that a mesh axis runs over, the one named last changes fastest.
Arguments:
- dipole_field: bfloat16 [2, 3, 16, 512, 256], P(None, None, 'zg', 'xy'), may hold values from -6 to 6
- material: int32 [16, 512, 2], P('zg', 'xy'), may hold values from 0 to 3
- alpha_table: float32 [4, 2, 3, 3], replicated, may hold values from -3 to 3
- green_spectrum: bfloat16 [2, 6, 32, 1024, 512], P(None, None, 'xy', None, 'zg'), may hold values from -6 to 6
- green_scale: float32 [6, 32], P(None, 'xy'), may hold values from 0.5 to 2
Outputs:
- scattered_field: bfloat16 [2, 3, 16, 512, 256], P(None, None, 'zg', 'xy')
The draws below stay inside these ranges and needn't reach their ends.
All inputs are finite; a program needn't handle non-finite values.
Results may differ from the reference program's by a relative error of at most 0.019.
Values may be sent and summed in bfloat16 or wider, within the bound.
A program may use at most 128 MiB of HBM per device.

```python
import math
import jax
import jax.numpy as jnp
from jax import lax

NZ = 16
NX = 512
NYW = 256
COLB = 128
NMAT = 4
LZ = 32
LX = 1024
LY = 512


def with_ends(values, key, smallest, largest):
    index_at = [jax.random.randint(jax.random.fold_in(key, axis), (), 0, length) for axis, length in enumerate(values.shape)]
    longest = values.shape.index(max(values.shape))
    beside = index_at[:longest] + [(index_at[longest] + 1) % values.shape[longest]] + index_at[longest + 1:]
    return values.at[tuple(index_at)].set(smallest).at[tuple(beside)].set(largest)


def shard_levels(key, shape, cuts, least, largest):
    factor_of = 1.0
    for dim, shards_of in cuts:
        draws = jax.random.uniform(jax.random.fold_in(jax.random.fold_in(key, 6), dim), (shards_of,), jnp.float32, least / len(cuts), largest / len(cuts))
        factor_of = factor_of * jnp.repeat(jnp.exp(draws), shape[dim] // shards_of).reshape((-1,) + (1,) * (len(shape) - 1 - dim))
    return factor_of


def normal_values(key, shape, scale, reach, cuts=(), kind=jnp.bfloat16):
    gain = shard_levels(key, shape, cuts, -0.22, 0.18) if cuts else 1.0
    drawn = jax.random.normal(key, shape, jnp.float32) * scale * gain
    return jnp.minimum(jnp.maximum(drawn, -reach), reach).astype(kind)


def setup_inputs(seed: int = 0) -> dict:
    key_list = jax.random.split(jax.random.key(seed), 6)
    dipole_field = normal_values(key_list[0], (2, 3, NZ, NX, NYW), 1.0, 6.0, ((2, 4), (3, 32)))
    material = with_ends(jax.random.randint(key_list[1], (NZ, NX, NYW // COLB), 0, NMAT), jax.random.fold_in(key_list[1], 1), 0, NMAT - 1).astype(jnp.int32)
    alpha_table = normal_values(key_list[2], (NMAT, 2, 3, 3), 0.5, 3.0, (), jnp.float32)
    green_spectrum = normal_values(key_list[3], (2, 6, LZ, LX, LY), 1.0, 6.0, ((2, 32), (4, 4)))
    green_scale = jnp.clip(jnp.exp(math.log(2.0) - 1.3862944 * jax.random.uniform(key_list[4], (6, LZ), jnp.float32) ** shard_levels(key_list[4], (6, LZ), ((1, 32),), -0.2, 0.2)), 0.5, 2.0)
    return {"dipole_field": dipole_field, "material": material, "alpha_table": alpha_table, "green_spectrum": green_spectrum, "green_scale": green_scale}


pairing = ((0, 3, 4), (3, 1, 5), (4, 5, 2))


def dft_table(count_in, count_out, length, direction):
    source = jnp.arange(count_in, dtype=jnp.int32)[:, None]
    target = jnp.arange(count_out, dtype=jnp.int32)[None, :]
    phases = ((source * target) % length).astype(jnp.float32) * (2.0 * math.pi / length)
    return jnp.cos(phases).astype(jnp.bfloat16), (direction * jnp.sin(phases)).astype(jnp.bfloat16)


def transform(spectrum, tables, form):
    cosine_table, sine_table = tables

    def contract(operand, matrix):
        return jnp.einsum(form, operand.astype(jnp.float32), matrix.astype(jnp.float32))

    out_real = contract(spectrum[0], cosine_table) - contract(spectrum[1], sine_table)
    out_imag = contract(spectrum[0], sine_table) + contract(spectrum[1], cosine_table)
    return jnp.stack([out_real, out_imag])


def moments_of(dipole_field, material, alpha_table):
    counts = alpha_table.shape[0]
    onehot = (material[None] == jnp.arange(counts, dtype=jnp.int32)[:, None, None, None]).astype(jnp.float32)
    tensors = jnp.einsum("mzxb,mrij->rijzxb", onehot, alpha_table.astype(jnp.float32))
    layout = dipole_field.shape
    blocks = material.shape[2]
    values = dipole_field.astype(jnp.float32).reshape(layout[0], layout[1], layout[2], layout[3], blocks, layout[4] // blocks)
    real_part = jnp.einsum("ijzxb,jzxbc->izxbc", tensors[0], values[0]) - jnp.einsum("ijzxb,jzxbc->izxbc", tensors[1], values[1])
    imag_part = jnp.einsum("ijzxb,jzxbc->izxbc", tensors[0], values[1]) + jnp.einsum("ijzxb,jzxbc->izxbc", tensors[1], values[0])
    return jnp.stack([real_part, imag_part]).reshape(layout).astype(jnp.bfloat16)


def spectral(spectrum, green_part, factors):
    weighted = green_part.astype(jnp.float32) * factors
    spectrum_real = spectrum[0].astype(jnp.float32)
    spectrum_imag = spectrum[1].astype(jnp.float32)
    reals = []
    imags = []
    for row_axis in range(3):
        total_real = jnp.zeros(spectrum_real.shape[1:], jnp.float32)
        total_imag = jnp.zeros(spectrum_real.shape[1:], jnp.float32)
        for col_axis in range(3):
            component = pairing[row_axis][col_axis]
            green_real = weighted[0, component]
            green_imag = weighted[1, component]
            total_real = total_real + green_real * spectrum_real[col_axis] - green_imag * spectrum_imag[col_axis]
            total_imag = total_imag + green_real * spectrum_imag[col_axis] + green_imag * spectrum_real[col_axis]
        reals.append(total_real)
        imags.append(total_imag)
    return jnp.stack([jnp.stack(reals), jnp.stack(imags)]).astype(jnp.bfloat16)


def reference(dipole_field, material, alpha_table, green_spectrum, green_scale):
    moments = moments_of(dipole_field, material, alpha_table)
    spectrum_y = transform(moments, dft_table(NYW, LY, LY, -1.0), "czxy,yk->czxk").astype(jnp.bfloat16)
    spectrum_z = transform(spectrum_y, dft_table(NZ, LZ, LZ, -1.0), "czxy,zk->ckxy").astype(jnp.bfloat16)

    def per_plane(members):
        spectrum_plane, green_plane, scale_plane = members
        spectrum_x = transform(spectrum_plane, dft_table(NX, LX, LX, -1.0), "cxy,xk->cky").astype(jnp.bfloat16)
        product = spectral(spectrum_x, green_plane, scale_plane[:, None, None])
        return transform(product, dft_table(LX, NX, LX, 1.0), "cky,kx->cxy").astype(jnp.bfloat16)

    planes = lax.map(per_plane, (jnp.moveaxis(spectrum_z, 2, 0), jnp.moveaxis(green_spectrum, 2, 0), jnp.transpose(green_scale)))
    back_x = jnp.moveaxis(planes, 0, 2)
    back_z = transform(back_x, dft_table(LZ, NZ, LZ, 1.0), "ckxy,kz->czxy").astype(jnp.bfloat16)
    back_y = transform(back_z, dft_table(LY, NYW, LY, 1.0), "czxk,ky->czxy")
    result = dipole_field.astype(jnp.float32) - back_y / float(LX * LY * LZ)
    return result.astype(jnp.bfloat16)
```

```python
import functools
import math

import jax
import jax.numpy as jnp
import ml_dtypes
import numpy as np
from jax import lax
from jax.experimental import pallas as pl
from jax.experimental.pallas import tpu as pltpu
from jax.sharding import PartitionSpec as P

MESH = pl.DeviceIdType.MESH
F32 = jnp.float32
BF16 = jnp.bfloat16

pairing = ((0, 3, 4), (3, 1, 5), (4, 5, 2))


def dft_table(count_in, count_out, length, direction):
    phases = (np.arange(count_in)[:, None] * np.arange(count_out)[None, :] % length).astype(np.float32)
    phases = phases * np.float32(2.0 * math.pi / length)
    cosine = np.cos(phases).astype(ml_dtypes.bfloat16).astype(np.float32)
    sine = (np.float32(direction) * np.sin(phases)).astype(ml_dtypes.bfloat16).astype(np.float32)
    return cosine, sine


def tables_of(rows_y, planes_z, rows_x, n_zg, n_xy):
    length_y, length_z, length_x = 2 * rows_y, 2 * planes_z, 2 * rows_x
    block_y = length_y // n_zg
    local_x = rows_x // n_xy
    eye = np.eye(local_x, dtype=np.float32)
    c, s = dft_table(rows_y, length_y, length_y, -1.0)
    full = np.block([[c, s], [-s, c]]).reshape(2 * rows_y, 2, n_zg, block_y)
    forward_y = full.transpose(0, 2, 1, 3).reshape(2 * rows_y, 2 * length_y)
    c, s = dft_table(planes_z, length_z, length_z, -1.0)
    forward_z = np.concatenate([np.kron(c.T, eye), np.kron(s.T, eye)], axis=1)
    c, s = dft_table(rows_x, length_x, length_x, -1.0)
    forward_x = np.concatenate([c.T, s.T], axis=1)
    c, s = dft_table(length_x, rows_x, length_x, 1.0)
    inverse_x = np.concatenate([c.T, s.T], axis=1)
    c, s = dft_table(length_z, planes_z, length_z, 1.0)
    inverse_z = np.concatenate([np.kron(c.T, eye), np.kron(s.T, eye)], axis=1)
    c, s = dft_table(length_y, rows_y, length_y, 1.0)
    full = np.block([[c, s], [-s, c]]).reshape(2, n_zg, block_y, 2 * rows_y)
    inverse_y = full.transpose(1, 0, 2, 3).reshape(2 * length_y, 2 * rows_y)
    return [
        np.ascontiguousarray(t).astype(ml_dtypes.bfloat16)
        for t in (forward_y, forward_z, forward_x, inverse_x, inverse_z, inverse_y)
    ]


def times_i(pair):
    half = pair.shape[1] // 2
    return jnp.concatenate([-pair[:, half:], pair[:, :half]], axis=1)


def stacked(pair):
    return jnp.concatenate([pair, times_i(pair)], axis=0)


def dot(a, b):
    return jnp.dot(a, b, preferred_element_type=F32)


def kernel(
    n_zg, n_xy, norm,
    field_hbm, material_ref, alpha_ref, green_hbm, scale_ref,
    ty_hbm, tz_hbm, tx_hbm, ux_hbm, uz_hbm, uy_hbm,
    out_ref,
    field, green, ty, tz, tx, ux, uz, uy,
    mom, a_send, a_recv, b_send, b_recv, spec, prod, c_send, c_recv, d_send, d_recv,
    load_sem, a_ss, a_rs, b_ss, b_rs, c_ss, c_rs, d_ss, d_rs,
):
    g = lax.axis_index("zg")
    q = lax.axis_index("xy")
    loads = [
        pltpu.make_async_copy(src, dst, load_sem.at[index])
        for index, (src, dst) in enumerate(
            (
                (field_hbm, field), (ty_hbm, ty), (tz_hbm, tz), (tx_hbm, tx),
                (green_hbm, green), (ux_hbm, ux), (uz_hbm, uz), (uy_hbm, uy),
            )
        )
    ]
    for load in loads:
        load.start()

    barrier = pltpu.get_barrier_semaphore()

    def greet_xy(step, carry):
        peer = lax.rem(q + step, n_xy)
        pl.semaphore_signal(barrier, inc=1, device_id=(g, peer), device_id_type=MESH)
        return carry

    def greet_zg(step, carry):
        peer = lax.rem(g + step, n_zg)
        pl.semaphore_signal(barrier, inc=1, device_id=(peer, q), device_id_type=MESH)
        return carry

    lax.fori_loop(1, n_xy, greet_xy, 0)
    lax.fori_loop(1, n_zg, greet_zg, 0)

    loads[0].wait()
    planes, rows, width = field.shape[2:]
    half = width // 2
    for z in range(planes):
        for b in range(2):
            lanes = slice(b * half, (b + 1) * half)
            which = jnp.broadcast_to(material_ref[z][:, b : b + 1], (rows, half))
            masks = [which == m for m in range(3)]

            def tensor(r, i, j):
                value = jnp.full((rows, half), alpha_ref[3, r, i, j], F32)
                for m in range(3):
                    value = jnp.where(masks[m], alpha_ref[m, r, i, j], value)
                return value

            values = [[field[r, j, z, :, lanes].astype(F32) for j in range(3)] for r in range(2)]
            for i in range(3):
                real = jnp.zeros((rows, half), F32)
                imag = jnp.zeros((rows, half), F32)
                for j in range(3):
                    t_re, t_im = tensor(0, i, j), tensor(1, i, j)
                    real = real + t_re * values[0][j] - t_im * values[1][j]
                    imag = imag + t_re * values[1][j] + t_im * values[0][j]
                start = (i * planes + z) * rows
                mom[start : start + rows, b * half : (b + 1) * half] = real.astype(BF16)
                mom[start : start + rows, width + b * half : width + (b + 1) * half] = imag.astype(BF16)

    def exchange(send, recv, ss, rs, index, axis):
        count, me = (n_zg, g) if axis == "zg" else (n_xy, q)

        def step_of(step, carry):
            peer = lax.rem(me + step, count)
            target = (peer, q) if axis == "zg" else (g, peer)
            pltpu.make_async_remote_copy(
                send.at[index, peer], recv.at[index, me], ss.at[index], rs.at[index],
                device_id=target, device_id_type=MESH,
            ).start()
            return carry

        lax.fori_loop(1, count, step_of, 0)
        recv[index, me] = send[index, me]

    def arrived(recv, rs, index):
        others = recv.at[index, pl.ds(0, recv.shape[1] - 1)]
        pltpu.make_async_copy(others, others, rs.at[index]).wait()

    loads[1].wait()
    spectrum = dot(mom[...], ty[...]).astype(BF16)
    plane_rows = planes * rows
    lanes2 = spectrum.shape[1] // n_zg
    for i in range(3):
        for p in range(n_zg):
            a_send[i, p] = spectrum[i * plane_rows : (i + 1) * plane_rows, p * lanes2 : (p + 1) * lanes2]
    pl.semaphore_wait(barrier, n_xy + n_zg - 2)
    for i in range(3):
        exchange(a_send, a_recv, a_ss, a_rs, i, "zg")

    loads[2].wait()
    for i in range(3):
        arrived(a_recv, a_rs, i)
        operand = a_recv[i].reshape(n_zg * plane_rows, lanes2)
        b_send[i] = dot(tz[...], stacked(operand)).astype(BF16).reshape(b_send.shape[1:])
        exchange(b_send, b_recv, b_ss, b_rs, i, "xy")

    loads[3].wait()
    rows_x = n_xy * rows

    def forward_x(i, carry):
        arrived(b_recv, b_rs, i)
        operand = b_recv[i].reshape(rows_x, lanes2)
        spec[i] = dot(tx[...], stacked(operand)).astype(BF16)
        return carry

    lax.fori_loop(0, 3, forward_x, 0)

    loads[4].wait()
    loads[5].wait()
    block = lanes2 // 2
    length_x = spec.shape[1]
    step_rows = 32
    for i in range(3):

        def product(step, carry):
            at = pl.ds(pl.multiple_of(step * step_rows, step_rows), step_rows)
            real = jnp.zeros((step_rows, block), F32)
            imag = jnp.zeros((step_rows, block), F32)
            for j in range(3):
                c = pairing[i][j]
                factor = scale_ref[c, 0]
                g_re = green[0, c, at, :].astype(F32) * factor
                g_im = green[1, c, at, :].astype(F32) * factor
                s_re = spec[j, at, :block].astype(F32)
                s_im = spec[j, at, block:].astype(F32)
                real = real + g_re * s_re - g_im * s_im
                imag = imag + g_re * s_im + g_im * s_re
            prod[at, :block] = real.astype(BF16)
            prod[at, block:] = imag.astype(BF16)
            return carry

        lax.fori_loop(0, length_x // step_rows, product, 0)
        c_send[i] = dot(ux[...], stacked(prod[...])).astype(BF16).reshape(c_send.shape[1:])
        exchange(c_send, c_recv, c_ss, c_rs, i, "xy")

    loads[6].wait()
    for i in range(3):
        arrived(c_recv, c_rs, i)
        operand = c_recv[i].reshape(rows_x, lanes2)
        d_send[i] = dot(uz[...], stacked(operand)).astype(BF16).reshape(d_send.shape[1:])
        exchange(d_send, d_recv, d_ss, d_rs, i, "zg")

    loads[7].wait()
    for i in range(3):
        arrived(d_recv, d_rs, i)
        operand = jnp.concatenate([d_recv[i, p] for p in range(n_zg)], axis=1)
        back = dot(operand, uy[...])
        for r in range(2):
            part = back[:, r * width : (r + 1) * width].reshape(planes, rows, width)
            out_ref[r, i] = (field[r, i].astype(F32) - part * norm).astype(BF16)

    for send, ss in ((a_send, a_ss), (b_send, b_ss), (c_send, c_ss), (d_send, d_ss)):
        for i in range(3):
            arrived(send, ss, i)


def on_device(dipole_field, material, alpha_table, green_spectrum, green_scale):
    n_zg = lax.axis_size("zg")
    n_xy = lax.axis_size("xy")
    _, _, planes, rows, width = dipole_field.shape
    planes_z, rows_x = planes * n_zg, rows * n_xy
    tables = tables_of(width, planes_z, rows_x, n_zg, n_xy)
    norm = 1.0 / float(8 * width * planes_z * rows_x)
    green = green_spectrum.reshape(green_spectrum.shape[:2] + green_spectrum.shape[3:])
    block = 2 * width // n_zg
    plane_rows = planes * rows
    dma = lambda n: pltpu.SemaphoreType.DMA((n,))
    over_zg = pltpu.VMEM((3, n_zg, plane_rows, 2 * block), BF16)
    over_xy = pltpu.VMEM((3, n_xy, rows, 2 * block), BF16)
    anywhere = pl.BlockSpec(memory_space=pl.ANY)
    vmem = pl.BlockSpec(memory_space=pltpu.VMEM)
    smem = pl.BlockSpec(memory_space=pltpu.SMEM)
    return pl.pallas_call(
        functools.partial(kernel, n_zg, n_xy, norm),
        out_shape=jax.ShapeDtypeStruct(dipole_field.shape, BF16),
        in_specs=[anywhere, vmem, smem, anywhere, smem] + [anywhere] * 6,
        out_specs=vmem,
        scratch_shapes=[
            pltpu.VMEM(dipole_field.shape, BF16),
            pltpu.VMEM(green.shape, BF16),
        ]
        + [pltpu.VMEM(t.shape, BF16) for t in tables]
        + [
            pltpu.VMEM((3 * plane_rows, 2 * width), BF16),
            over_zg, over_zg, over_xy, over_xy,
            pltpu.VMEM((3, 2 * rows_x, 2 * block), BF16),
            pltpu.VMEM((2 * rows_x, 2 * block), BF16),
            over_xy, over_xy, over_zg, over_zg,
            dma(8),
        ]
        + [dma(3)] * 8,
        compiler_params=pltpu.CompilerParams(
            collective_id=0, has_side_effects=True, vmem_limit_bytes=56 * 1024 * 1024
        ),
        cost_estimate=pl.CostEstimate(flops=5_000_000_000, bytes_accessed=12_000_000, transcendentals=0),
    )(dipole_field, material, alpha_table, green, green_scale, *[jnp.asarray(t) for t in tables])


def solution(mesh):
    return jax.shard_map(
        on_device,
        mesh=mesh,
        in_specs=(
            P(None, None, "zg", "xy", None),
            P("zg", "xy", None),
            P(),
            P(None, None, "xy", None, "zg"),
            P(None, "xy"),
        ),
        out_specs=P(None, None, "zg", "xy", None),
        check_vma=False,
    )
```

```python
import functools
import math

import jax
import jax.numpy as jnp
import ml_dtypes
import numpy as np
from jax import lax
from jax.experimental import pallas as pl
from jax.experimental.pallas import tpu as pltpu
from jax.sharding import PartitionSpec as P

MESH = pl.DeviceIdType.MESH
F32 = jnp.float32
BF16 = jnp.bfloat16

pairing = ((0, 3, 4), (3, 1, 5), (4, 5, 2))


def dft_table(count_in, count_out, length, direction):
    phases = (np.arange(count_in)[:, None] * np.arange(count_out)[None, :] % length).astype(np.float32)
    phases = phases * np.float32(2.0 * math.pi / length)
    cosine = np.cos(phases).astype(ml_dtypes.bfloat16).astype(np.float32)
    sine = (np.float32(direction) * np.sin(phases)).astype(ml_dtypes.bfloat16).astype(np.float32)
    return cosine, sine


def tables_of(rows_y, planes_z, rows_x, n_zg, n_xy):
    length_y, length_z, length_x = 2 * rows_y, 2 * planes_z, 2 * rows_x
    block_y = length_y // n_zg
    local_x = rows_x // n_xy
    eye = np.eye(local_x, dtype=np.float32)
    c, s = dft_table(rows_y, length_y, length_y, -1.0)
    full = np.block([[c, s], [-s, c]]).reshape(2 * rows_y, 2, n_zg, block_y)
    forward_y = full.transpose(0, 2, 1, 3).reshape(2 * rows_y, 2 * length_y)
    c, s = dft_table(planes_z, length_z, length_z, -1.0)
    forward_z = np.concatenate([np.kron(c.T, eye), np.kron(s.T, eye)], axis=1)
    c, s = dft_table(rows_x, length_x, length_x, -1.0)
    forward_x = np.concatenate([c.T, s.T], axis=1)
    c, s = dft_table(length_x, rows_x, length_x, 1.0)
    inverse_x = np.concatenate([c.T, s.T], axis=1)
    c, s = dft_table(length_z, planes_z, length_z, 1.0)
    inverse_z = np.concatenate([np.kron(c.T, eye), np.kron(s.T, eye)], axis=1)
    c, s = dft_table(length_y, rows_y, length_y, 1.0)
    full = np.block([[c, s], [-s, c]]).reshape(2, n_zg, block_y, 2 * rows_y)
    inverse_y = full.transpose(1, 0, 2, 3).reshape(2 * length_y, 2 * rows_y)
    return [
        np.ascontiguousarray(t).astype(ml_dtypes.bfloat16)
        for t in (forward_y, forward_z, forward_x, inverse_x, inverse_z, inverse_y)
    ]


def times_i(pair):
    half = pair.shape[1] // 2
    return jnp.concatenate([-pair[:, half:], pair[:, :half]], axis=1)


def stacked(pair):
    return jnp.concatenate([pair, times_i(pair)], axis=0)


def dot(a, b):
    return jnp.dot(a, b, preferred_element_type=F32)


def kernel(
    n_zg, n_xy, norm,
    field_hbm, material_ref, alpha_ref, green_hbm, scale_ref,
    ty_hbm, tz_hbm, tx_hbm, ux_hbm, uz_hbm, uy_hbm,
    out_hbm,
    field, green, ty, tz, tx, ux, uz, uy,
    mom, a_send, a_recv, b_send, b_recv, spec, weighted, total, prod, c_send, c_recv, d_send, d_recv, out,
    load_sem, store_sem, a_ss, a_rs, b_ss, b_rs, c_ss, c_rs, d_ss, d_rs,
):
    g = lax.axis_index("zg")
    q = lax.axis_index("xy")
    loads = [
        pltpu.make_async_copy(src, dst, load_sem.at[index])
        for index, (src, dst) in enumerate(
            (
                (field_hbm, field), (ty_hbm, ty), (tz_hbm, tz), (tx_hbm, tx),
                (green_hbm, green), (ux_hbm, ux), (uz_hbm, uz), (uy_hbm, uy),
            )
        )
    ]
    for load in loads[:3]:
        load.start()

    barrier = pltpu.get_barrier_semaphore()

    def greet_xy(step, carry):
        peer = lax.rem(q + step, n_xy)
        pl.semaphore_signal(barrier, inc=1, device_id=(g, peer), device_id_type=MESH)
        return carry

    def greet_zg(step, carry):
        peer = lax.rem(g + step, n_zg)
        pl.semaphore_signal(barrier, inc=1, device_id=(peer, q), device_id_type=MESH)
        return carry

    lax.fori_loop(1, n_xy, greet_xy, 0)
    lax.fori_loop(1, n_zg, greet_zg, 0)

    loads[0].wait()
    planes, rows, width = field.shape[2:]
    half = width // 2
    diagonal = lax.broadcasted_iota(jnp.int32, (rows, rows), 0) == lax.broadcasted_iota(jnp.int32, (rows, rows), 1)
    for z in range(planes):
        for b in range(2):
            lanes = slice(b * half, (b + 1) * half)
            across = jnp.broadcast_to(material_ref[z, b : b + 1, :].astype(F32), (rows, rows))
            which = jnp.sum(jnp.where(diagonal, across, 0.0), axis=1, keepdims=True)
            which = jnp.broadcast_to(which, (rows, half))
            masks = [which == float(m) for m in range(3)]

            def tensor(r, i, j):
                value = jnp.full((rows, half), alpha_ref[i, j, r, 3], F32)
                for m in range(3):
                    value = jnp.where(masks[m], alpha_ref[i, j, r, m], value)
                return value

            values = [[field[r, j, z, :, lanes].astype(F32) for j in range(3)] for r in range(2)]
            for i in range(3):
                real = jnp.zeros((rows, half), F32)
                imag = jnp.zeros((rows, half), F32)
                for j in range(3):
                    t_re, t_im = tensor(0, i, j), tensor(1, i, j)
                    real = real + t_re * values[0][j] - t_im * values[1][j]
                    imag = imag + t_re * values[1][j] + t_im * values[0][j]
                start = (i * planes + z) * rows
                mom[start : start + rows, b * half : (b + 1) * half] = real.astype(BF16)
                mom[start : start + rows, width + b * half : width + (b + 1) * half] = imag.astype(BF16)

    def exchange(send, recv, ss, rs, index, axis):
        count, me = (n_zg, g) if axis == "zg" else (n_xy, q)

        def step_of(step, carry):
            peer = lax.rem(me + step, count)
            target = (peer, q) if axis == "zg" else (g, peer)
            pltpu.make_async_remote_copy(
                send.at[index, peer], recv.at[index, me], ss.at[index], rs.at[index],
                device_id=target, device_id_type=MESH,
            ).start()
            return carry

        lax.fori_loop(1, count, step_of, 0)
        recv[index, me] = send[index, me]

    def arrived(recv, rs, index):
        others = recv.at[index, pl.ds(0, recv.shape[1] - 1)]
        pltpu.make_async_copy(others, others, rs.at[index]).wait()

    loads[1].wait()
    spectrum = dot(mom[...], ty[...]).astype(BF16)
    plane_rows = planes * rows
    lanes2 = spectrum.shape[1] // n_zg
    for i in range(3):
        for p in range(n_zg):
            a_send[i, p] = spectrum[i * plane_rows : (i + 1) * plane_rows, p * lanes2 : (p + 1) * lanes2]
    pl.semaphore_wait(barrier, n_xy + n_zg - 2)
    for i in range(3):
        exchange(a_send, a_recv, a_ss, a_rs, i, "zg")
    for load in loads[3:]:
        load.start()

    loads[2].wait()
    for i in range(3):
        arrived(a_recv, a_rs, i)
        operand = a_recv[i].reshape(n_zg * plane_rows, lanes2)
        b_send[i] = dot(tz[...], stacked(operand)).astype(BF16).reshape(b_send.shape[1:])
        exchange(b_send, b_recv, b_ss, b_rs, i, "xy")

    block = lanes2 // 2
    length_x = prod.shape[0]
    step_rows = 32
    loads[4].wait()

    def weigh(step, carry):
        at = pl.ds(pl.multiple_of(step * step_rows, step_rows), step_rows)
        for c in range(6):
            for r in range(2):
                weighted[r, c, at, :] = green[r, c, at, :].astype(F32) * scale_ref[0, c]
        return carry

    lax.fori_loop(0, length_x // step_rows, weigh, 0)

    loads[3].wait()
    loads[5].wait()
    rows_x = n_xy * rows

    def terms(spectrum, at, i, j):
        c = pairing[i][j]
        g_re, g_im = weighted[0, c, at, :], weighted[1, c, at, :]
        s_re, s_im = spectrum[:, :block], spectrum[:, block:]
        return g_re * s_re - g_im * s_im, g_re * s_im + g_im * s_re

    for j in range(3):
        arrived(b_recv, b_rs, j)
        operand = b_recv[j].reshape(rows_x, lanes2)
        spec[...] = dot(tx[...], stacked(operand)).astype(BF16)

        def accumulate(step, carry, i, final):
            at = pl.ds(pl.multiple_of(step * step_rows, step_rows), step_rows)
            spectrum = spec[at, :].astype(F32)
            real, imag = terms(spectrum, at, i, j)
            if j > 0:
                real = real + total[i, at, :block]
                imag = imag + total[i, at, block:]
            if final:
                prod[at, :block] = real.astype(BF16)
                prod[at, block:] = imag.astype(BF16)
            else:
                total[i, at, :block] = real
                total[i, at, block:] = imag
            return carry

        for i in range(3):
            final = j == 2
            lax.fori_loop(0, length_x // step_rows, functools.partial(accumulate, i=i, final=final), 0)
            if final:
                c_send[i] = dot(ux[...], stacked(prod[...])).astype(BF16).reshape(c_send.shape[1:])
                exchange(c_send, c_recv, c_ss, c_rs, i, "xy")

    loads[6].wait()
    for i in range(3):
        arrived(c_recv, c_rs, i)
        operand = c_recv[i].reshape(rows_x, lanes2)
        d_send[i] = dot(uz[...], stacked(operand)).astype(BF16).reshape(d_send.shape[1:])
        exchange(d_send, d_recv, d_ss, d_rs, i, "zg")

    def store_of(i):
        return pltpu.make_async_copy(out.at[:, i], out_hbm.at[:, i], store_sem.at[i])

    loads[7].wait()
    for i in range(3):
        arrived(d_recv, d_rs, i)
        operand = jnp.concatenate([d_recv[i, p] for p in range(n_zg)], axis=1)
        back = dot(operand, uy[...])
        for r in range(2):
            part = back[:, r * width : (r + 1) * width].reshape(planes, rows, width)
            out[r, i] = (field[r, i].astype(F32) - part * norm).astype(BF16)
        store_of(i).start()

    for send, ss in ((a_send, a_ss), (b_send, b_ss), (c_send, c_ss), (d_send, d_ss)):
        for i in range(3):
            arrived(send, ss, i)
    for i in range(3):
        store_of(i).wait()


def on_device(dipole_field, material, alpha_table, green_spectrum, green_scale):
    n_zg = lax.axis_size("zg")
    n_xy = lax.axis_size("xy")
    _, _, planes, rows, width = dipole_field.shape
    planes_z, rows_x = planes * n_zg, rows * n_xy
    tables = tables_of(width, planes_z, rows_x, n_zg, n_xy)
    norm = 1.0 / float(8 * width * planes_z * rows_x)
    green = green_spectrum.reshape(green_spectrum.shape[:2] + green_spectrum.shape[3:])
    material = material.transpose(0, 2, 1)
    alpha_table = alpha_table.transpose(2, 3, 1, 0)
    green_scale = green_scale.transpose(1, 0)
    block = 2 * width // n_zg
    plane_rows = planes * rows
    dma = lambda n: pltpu.SemaphoreType.DMA((n,))
    over_zg = pltpu.VMEM((3, n_zg, plane_rows, 2 * block), BF16)
    over_xy = pltpu.VMEM((3, n_xy, rows, 2 * block), BF16)
    anywhere = pl.BlockSpec(memory_space=pl.ANY)
    vmem = pl.BlockSpec(memory_space=pltpu.VMEM)
    smem = pl.BlockSpec(memory_space=pltpu.SMEM)
    return pl.pallas_call(
        functools.partial(kernel, n_zg, n_xy, norm),
        out_shape=jax.ShapeDtypeStruct(dipole_field.shape, BF16),
        in_specs=[anywhere, vmem, smem, anywhere, smem] + [anywhere] * 6,
        out_specs=anywhere,
        scratch_shapes=[
            pltpu.VMEM(dipole_field.shape, BF16),
            pltpu.VMEM(green.shape, BF16),
        ]
        + [pltpu.VMEM(t.shape, BF16) for t in tables]
        + [
            pltpu.VMEM((3 * plane_rows, 2 * width), BF16),
            over_zg, over_zg, over_xy, over_xy,
            pltpu.VMEM((2 * rows_x, 2 * block), BF16),
            pltpu.VMEM(green.shape, F32),
            pltpu.VMEM((3, 2 * rows_x, 2 * block), F32),
            pltpu.VMEM((2 * rows_x, 2 * block), BF16),
            over_xy, over_xy, over_zg, over_zg,
            pltpu.VMEM(dipole_field.shape, BF16),
            dma(8), dma(3),
        ]
        + [dma(3)] * 8,
        compiler_params=pltpu.CompilerParams(
            collective_id=0, has_side_effects=True, vmem_limit_bytes=56 * 1024 * 1024
        ),
        cost_estimate=pl.CostEstimate(flops=5_000_000_000, bytes_accessed=12_000_000, transcendentals=0),
    )(dipole_field, material, alpha_table, green, green_scale, *[jnp.asarray(t) for t in tables])


def solution(mesh):
    return jax.shard_map(
        on_device,
        mesh=mesh,
        in_specs=(
            P(None, None, "zg", "xy", None),
            P("zg", "xy", None),
            P(),
            P(None, None, "xy", None, "zg"),
            P(None, "xy"),
        ),
        out_specs=P(None, None, "zg", "xy", None),
        check_vma=False,
    )
```

```python
import functools
import math

import jax
import jax.numpy as jnp
import ml_dtypes
import numpy as np
from jax import lax
from jax.experimental import pallas as pl
from jax.experimental.pallas import tpu as pltpu
from jax.sharding import PartitionSpec as P

MESH = pl.DeviceIdType.MESH
F32 = jnp.float32
BF16 = jnp.bfloat16

pairing = ((0, 3, 4), (3, 1, 5), (4, 5, 2))


def dft_table(count_in, count_out, length, direction):
    phases = (np.arange(count_in)[:, None] * np.arange(count_out)[None, :] % length).astype(np.float32)
    phases = phases * np.float32(2.0 * math.pi / length)
    cosine = np.cos(phases).astype(ml_dtypes.bfloat16).astype(np.float32)
    sine = (np.float32(direction) * np.sin(phases)).astype(ml_dtypes.bfloat16).astype(np.float32)
    return cosine, sine


def tables_of(rows_y, planes_z, rows_x, n_zg, n_xy):
    length_y, length_z, length_x = 2 * rows_y, 2 * planes_z, 2 * rows_x
    block_y = length_y // n_zg
    local_x = rows_x // n_xy
    eye = np.eye(local_x, dtype=np.float32)
    c, s = dft_table(rows_y, length_y, length_y, -1.0)
    full = np.block([[c, s], [-s, c]]).reshape(2 * rows_y, 2, n_zg, block_y)
    forward_y = full.transpose(0, 2, 1, 3).reshape(2 * rows_y, 2 * length_y)
    c, s = dft_table(planes_z, length_z, length_z, -1.0)
    forward_z = np.concatenate([np.kron(c.T, eye), np.kron(s.T, eye)], axis=1)
    c, s = dft_table(rows_x, length_x, length_x, -1.0)
    forward_x = np.concatenate([c.T, s.T], axis=1)
    c, s = dft_table(length_x, rows_x, length_x, 1.0)
    inverse_x = np.concatenate([c.T, s.T], axis=1)
    c, s = dft_table(length_z, planes_z, length_z, 1.0)
    inverse_z = np.concatenate([np.kron(c.T, eye), np.kron(s.T, eye)], axis=1)
    c, s = dft_table(length_y, rows_y, length_y, 1.0)
    full = np.block([[c, s], [-s, c]]).reshape(2, n_zg, block_y, 2 * rows_y)
    inverse_y = full.transpose(1, 0, 2, 3).reshape(2 * length_y, 2 * rows_y)
    return [
        np.ascontiguousarray(t).astype(ml_dtypes.bfloat16)
        for t in (forward_y, forward_z, forward_x, inverse_x, inverse_z, inverse_y)
    ]


def times_i(pair):
    half = pair.shape[1] // 2
    return jnp.concatenate([-pair[:, half:], pair[:, :half]], axis=1)


def stacked(pair):
    return jnp.concatenate([pair, times_i(pair)], axis=0)


def far_first(d):
    return 2 + d + (d // 2) * (1 - 2 * d)


def dot(a, b):
    return jnp.dot(a, b, preferred_element_type=F32)


def kernel(
    n_zg, n_xy, norm,
    field_hbm, material_ref, alpha_ref, green_hbm, scale_ref,
    ty_hbm, tz_hbm, tx_hbm, ux_hbm, uz_hbm, uy_hbm,
    out_hbm,
    field, green, ty, tz, tx, ux, uz, uy,
    mom, a_send, a_recv, b_send, b_recv, spec, weighted, total, prod, c_send, c_recv, d_send, d_recv, out,
    load_sem, store_sem, a_ss, a_rs, b_ss, b_rs, c_ss, c_rs, d_ss, d_rs,
):
    g = lax.axis_index("zg")
    q = lax.axis_index("xy")
    loads = [
        pltpu.make_async_copy(src, dst, load_sem.at[index])
        for index, (src, dst) in enumerate(
            (
                (field_hbm, field), (ty_hbm, ty), (tz_hbm, tz), (tx_hbm, tx),
                (green_hbm, green), (ux_hbm, ux), (uz_hbm, uz), (uy_hbm, uy),
            )
        )
    ]
    for load in loads[:3]:
        load.start()

    barrier = pltpu.get_barrier_semaphore()

    def greet_xy(step, carry):
        peer = lax.rem(q + step, n_xy)
        pl.semaphore_signal(barrier, inc=1, device_id=(g, peer), device_id_type=MESH)
        return carry

    def greet_zg(step, carry):
        peer = lax.rem(g + step, n_zg)
        pl.semaphore_signal(barrier, inc=1, device_id=(peer, q), device_id_type=MESH)
        return carry

    lax.fori_loop(1, n_xy, greet_xy, 0)
    lax.fori_loop(1, n_zg, greet_zg, 0)

    loads[0].wait()
    planes, rows, width = field.shape[2:]
    half = width // 2
    diagonal = lax.broadcasted_iota(jnp.int32, (rows, rows), 0) == lax.broadcasted_iota(jnp.int32, (rows, rows), 1)
    def moments_of_plane(z, carry):
        for b in range(2):
            lanes = slice(b * half, (b + 1) * half)
            across = jnp.broadcast_to(material_ref[z, b : b + 1, :].astype(F32), (rows, rows))
            which = jnp.sum(jnp.where(diagonal, across, 0.0), axis=1, keepdims=True)
            which = jnp.broadcast_to(which, (rows, half))
            masks = [which == float(m) for m in range(3)]

            def tensor(r, i, j):
                value = jnp.full((rows, half), alpha_ref[i, j, r, 3], F32)
                for m in range(3):
                    value = jnp.where(masks[m], alpha_ref[i, j, r, m], value)
                return value

            values = [[field[r, j, z, :, lanes].astype(F32) for j in range(3)] for r in range(2)]
            for i in range(3):
                real = jnp.zeros((rows, half), F32)
                imag = jnp.zeros((rows, half), F32)
                for j in range(3):
                    t_re, t_im = tensor(0, i, j), tensor(1, i, j)
                    real = real + t_re * values[0][j] - t_im * values[1][j]
                    imag = imag + t_re * values[1][j] + t_im * values[0][j]
                mom[i, z, :, b * half : (b + 1) * half] = real.astype(BF16)
                mom[i, z, :, width + b * half : width + (b + 1) * half] = imag.astype(BF16)
        return carry

    lax.fori_loop(0, planes, moments_of_plane, 0)

    def exchange(send, recv, ss, rs, index, axis):
        count, me = (n_zg, g) if axis == "zg" else (n_xy, q)

        def step_of(step, carry):
            if axis == "xy" and count == 32:
                x, y, z = lax.rem(q, 4), lax.rem(q // 4, 4), q // 16
                k = step - 1
                peer_x = lax.rem(x + far_first(lax.rem(k, 4)), 4)
                peer_y = lax.rem(y + far_first(lax.rem(k // 4, 4)), 4)
                peer_z = lax.rem(z + 1 - k // 16, 2)
                peer = peer_z * 16 + peer_y * 4 + peer_x
            else:
                peer = lax.rem(me + step, count)
            target = (peer, q) if axis == "zg" else (g, peer)
            pltpu.make_async_remote_copy(
                send.at[index, peer], recv.at[index, me], ss.at[index], rs.at[index],
                device_id=target, device_id_type=MESH,
            ).start()
            return carry

        lax.fori_loop(1, count, step_of, 0)
        recv[index, me] = send[index, me]

    def arrived(recv, rs, index):
        others = recv.at[index, pl.ds(0, recv.shape[1] - 1)]
        pltpu.make_async_copy(others, others, rs.at[index]).wait()

    loads[1].wait()
    spectrum = dot(mom[...].reshape(3 * planes * rows, 2 * width), ty[...]).astype(BF16)
    plane_rows = planes * rows
    lanes2 = spectrum.shape[1] // n_zg
    for i in range(3):
        for p in range(n_zg):
            a_send[i, p] = spectrum[i * plane_rows : (i + 1) * plane_rows, p * lanes2 : (p + 1) * lanes2]
    pl.semaphore_wait(barrier, n_xy + n_zg - 2)
    for i in range(3):
        exchange(a_send, a_recv, a_ss, a_rs, i, "zg")
    for load in loads[3:]:
        load.start()

    loads[2].wait()

    def forward_z(i, carry):
        arrived(a_recv, a_rs, i)
        operand = a_recv[i].reshape(n_zg * plane_rows, lanes2)
        b_send[i] = dot(tz[...], stacked(operand)).astype(BF16).reshape(b_send.shape[1:])
        exchange(b_send, b_recv, b_ss, b_rs, i, "xy")
        return carry

    lax.fori_loop(0, 3, forward_z, 0)

    block = lanes2 // 2
    length_x = prod.shape[0]
    step_rows = 128
    loads[4].wait()

    def weigh(step, carry):
        at = pl.ds(pl.multiple_of(step * step_rows, step_rows), step_rows)
        for c in range(6):
            for r in range(2):
                weighted[r, c, at, :] = green[r, c, at, :].astype(F32) * scale_ref[0, c]
        for i in range(3):
            total[i, at, :] = jnp.zeros((step_rows, lanes2), F32)
        return carry

    lax.fori_loop(0, length_x // step_rows, weigh, 0)

    loads[3].wait()
    loads[5].wait()
    rows_x = n_xy * rows

    def added(i, j, at):
        c = jnp.where(i == j, i, i + j + 2)
        spectrum = spec[at, :].astype(F32)
        s_re, s_im = spectrum[:, :block], spectrum[:, block:]
        g_re, g_im = weighted[0, c, at, :], weighted[1, c, at, :]
        real = total[i, at, :block] + g_re * s_re - g_im * s_im
        imag = total[i, at, block:] + g_re * s_im + g_im * s_re
        return real, imag

    def forward_x(j, carry):
        arrived(b_recv, b_rs, j)
        operand = b_recv[j].reshape(rows_x, lanes2)
        spec[...] = dot(tx[...], stacked(operand)).astype(BF16)

        def accumulate(step, carry):
            at = pl.ds(pl.multiple_of(step * step_rows, step_rows), step_rows)
            for i in range(3):
                real, imag = added(i, j, at)
                total[i, at, :block] = real
                total[i, at, block:] = imag
            return carry

        return lax.fori_loop(0, jnp.where(j < 2, length_x // step_rows, 0), accumulate, carry)

    lax.fori_loop(0, 3, forward_x, 0)

    def inverse_x(i, carry):
        def finish(step, carry):
            at = pl.ds(pl.multiple_of(step * step_rows, step_rows), step_rows)
            real, imag = added(i, 2, at)
            prod[at, :block] = real.astype(BF16)
            prod[at, block:] = imag.astype(BF16)
            return carry

        lax.fori_loop(0, length_x // step_rows, finish, 0)
        c_send[i] = dot(ux[...], stacked(prod[...])).astype(BF16).reshape(c_send.shape[1:])
        exchange(c_send, c_recv, c_ss, c_rs, i, "xy")
        return carry

    lax.fori_loop(0, 3, inverse_x, 0)

    loads[6].wait()

    def inverse_z(i, carry):
        arrived(c_recv, c_rs, i)
        operand = c_recv[i].reshape(rows_x, lanes2)
        d_send[i] = dot(uz[...], stacked(operand)).astype(BF16).reshape(d_send.shape[1:])
        exchange(d_send, d_recv, d_ss, d_rs, i, "zg")
        return carry

    lax.fori_loop(0, 3, inverse_z, 0)

    def store_of(i):
        return pltpu.make_async_copy(out.at[:, i], out_hbm.at[:, i], store_sem.at[i])

    loads[7].wait()
    def inverse_y(i, carry):
        arrived(d_recv, d_rs, i)
        operand = jnp.concatenate([d_recv[i, p] for p in range(n_zg)], axis=1)
        back = dot(operand, uy[...])
        for r in range(2):
            part = back[:, r * width : (r + 1) * width].reshape(planes, rows, width)
            out[r, i] = (field[r, i].astype(F32) - part * norm).astype(BF16)
        store_of(i).start()
        return carry

    lax.fori_loop(0, 3, inverse_y, 0)

    for send, ss in ((a_send, a_ss), (b_send, b_ss), (c_send, c_ss), (d_send, d_ss)):
        for i in range(3):
            arrived(send, ss, i)
    for i in range(3):
        store_of(i).wait()


def on_device(dipole_field, material, alpha_table, green_spectrum, green_scale):
    n_zg = lax.axis_size("zg")
    n_xy = lax.axis_size("xy")
    _, _, planes, rows, width = dipole_field.shape
    planes_z, rows_x = planes * n_zg, rows * n_xy
    tables = tables_of(width, planes_z, rows_x, n_zg, n_xy)
    norm = 1.0 / float(8 * width * planes_z * rows_x)
    green = green_spectrum.reshape(green_spectrum.shape[:2] + green_spectrum.shape[3:])
    material = material.transpose(0, 2, 1)
    alpha_table = alpha_table.transpose(2, 3, 1, 0)
    green_scale = green_scale.transpose(1, 0)
    block = 2 * width // n_zg
    plane_rows = planes * rows
    dma = lambda n: pltpu.SemaphoreType.DMA((n,))
    over_zg = pltpu.VMEM((3, n_zg, plane_rows, 2 * block), BF16)
    over_xy = pltpu.VMEM((3, n_xy, rows, 2 * block), BF16)
    anywhere = pl.BlockSpec(memory_space=pl.ANY)
    vmem = pl.BlockSpec(memory_space=pltpu.VMEM)
    smem = pl.BlockSpec(memory_space=pltpu.SMEM)
    return pl.pallas_call(
        functools.partial(kernel, n_zg, n_xy, norm),
        out_shape=jax.ShapeDtypeStruct(dipole_field.shape, BF16),
        in_specs=[anywhere, vmem, smem, anywhere, smem] + [anywhere] * 6,
        out_specs=anywhere,
        scratch_shapes=[
            pltpu.VMEM(dipole_field.shape, BF16),
            pltpu.VMEM(green.shape, BF16),
        ]
        + [pltpu.VMEM(t.shape, BF16) for t in tables]
        + [
            pltpu.VMEM((3, planes, rows, 2 * width), BF16),
            over_zg, over_zg, over_xy, over_xy,
            pltpu.VMEM((2 * rows_x, 2 * block), BF16),
            pltpu.VMEM(green.shape, F32),
            pltpu.VMEM((3, 2 * rows_x, 2 * block), F32),
            pltpu.VMEM((2 * rows_x, 2 * block), BF16),
            over_xy, over_xy, over_zg, over_zg,
            pltpu.VMEM(dipole_field.shape, BF16),
            dma(8), dma(3),
        ]
        + [dma(3)] * 8,
        compiler_params=pltpu.CompilerParams(
            collective_id=0, has_side_effects=True, vmem_limit_bytes=56 * 1024 * 1024
        ),
        cost_estimate=pl.CostEstimate(flops=5_000_000_000, bytes_accessed=12_000_000, transcendentals=0),
    )(dipole_field, material, alpha_table, green, green_scale, *[jnp.asarray(t) for t in tables])


def solution(mesh):
    return jax.shard_map(
        on_device,
        mesh=mesh,
        in_specs=(
            P(None, None, "zg", "xy", None),
            P("zg", "xy", None),
            P(),
            P(None, None, "xy", None, "zg"),
            P(None, "xy"),
        ),
        out_specs=P(None, None, "zg", "xy", None),
        check_vma=False,
    )
```

```python
import functools
import math

import jax
import jax.numpy as jnp
import ml_dtypes
import numpy as np
from jax import lax
from jax.experimental import pallas as pl
from jax.experimental.pallas import tpu as pltpu
from jax.sharding import PartitionSpec as P

MESH = pl.DeviceIdType.MESH
F32 = jnp.float32
BF16 = jnp.bfloat16

pairing = ((0, 3, 4), (3, 1, 5), (4, 5, 2))


def dft_table(count_in, count_out, length, direction):
    phases = (np.arange(count_in)[:, None] * np.arange(count_out)[None, :] % length).astype(np.float32)
    phases = phases * np.float32(2.0 * math.pi / length)
    cosine = np.cos(phases).astype(ml_dtypes.bfloat16).astype(np.float32)
    sine = (np.float32(direction) * np.sin(phases)).astype(ml_dtypes.bfloat16).astype(np.float32)
    return cosine, sine


def tables_of(rows_y, planes_z, rows_x, n_zg, n_xy):
    length_y, length_z, length_x = 2 * rows_y, 2 * planes_z, 2 * rows_x
    block_y = length_y // n_zg
    local_x = rows_x // n_xy
    eye = np.eye(local_x, dtype=np.float32)
    c, s = dft_table(rows_y, length_y, length_y, -1.0)
    full = np.block([[c, s], [-s, c]]).reshape(2 * rows_y, 2, n_zg, block_y)
    forward_y = full.transpose(0, 2, 1, 3).reshape(2 * rows_y, 2 * length_y)
    c, s = dft_table(planes_z, length_z, length_z, -1.0)
    forward_z = np.concatenate([np.kron(c.T, eye), np.kron(s.T, eye)], axis=1)
    c, s = dft_table(rows_x, length_x, length_x, -1.0)
    forward_x = np.concatenate([c.T, s.T], axis=1)
    c, s = dft_table(length_x, rows_x, length_x, 1.0)
    inverse_x = np.concatenate([c.T, s.T], axis=1)
    c, s = dft_table(length_z, planes_z, length_z, 1.0)
    inverse_z = np.concatenate([np.kron(c.T, eye), np.kron(s.T, eye)], axis=1)
    c, s = dft_table(length_y, rows_y, length_y, 1.0)
    full = np.block([[c, s], [-s, c]]).reshape(2, n_zg, block_y, 2 * rows_y)
    inverse_y = full.transpose(1, 0, 2, 3).reshape(2 * length_y, 2 * rows_y)
    return [
        np.ascontiguousarray(t).astype(ml_dtypes.bfloat16)
        for t in (forward_y, forward_z, forward_x, inverse_x, inverse_z, inverse_y)
    ]


def times_i(pair):
    half = pair.shape[1] // 2
    return jnp.concatenate([-pair[:, half:], pair[:, :half]], axis=1)


def stacked(pair):
    return jnp.concatenate([pair, times_i(pair)], axis=0)


def far_first(d):
    return 2 + d + (d // 2) * (1 - 2 * d)


def dot(a, b):
    return jnp.dot(a, b, preferred_element_type=F32)


def kernel(
    n_zg, n_xy, norm,
    field_hbm, material_ref, alpha_ref, green_hbm, scale_ref,
    ty_hbm, tz_hbm, tx_hbm, ux_hbm, uz_hbm, uy_hbm,
    out,
    field, green, ty, tz, tx, ux, uz, uy,
    mom, a_send, a_recv, b_send, b_recv, spec, weighted, total, prod, c_send, c_recv, d_send, d_recv,
    load_sem, a_ss, a_rs, b_ss, b_rs, c_ss, c_rs, d_ss, d_rs,
):
    g = lax.axis_index("zg")
    q = lax.axis_index("xy")
    loads = [
        pltpu.make_async_copy(src, dst, load_sem.at[index])
        for index, (src, dst) in enumerate(
            (
                (field_hbm, field), (ty_hbm, ty), (tz_hbm, tz), (tx_hbm, tx),
                (green_hbm, green), (ux_hbm, ux), (uz_hbm, uz), (uy_hbm, uy),
            )
        )
    ]
    for load in loads[:3]:
        load.start()

    barrier = pltpu.get_barrier_semaphore()

    def greet_xy(step, carry):
        peer = lax.rem(q + step, n_xy)
        pl.semaphore_signal(barrier, inc=1, device_id=(g, peer), device_id_type=MESH)
        return carry

    def greet_zg(step, carry):
        peer = lax.rem(g + step, n_zg)
        pl.semaphore_signal(barrier, inc=1, device_id=(peer, q), device_id_type=MESH)
        return carry

    lax.fori_loop(1, n_xy, greet_xy, 0)
    lax.fori_loop(1, n_zg, greet_zg, 0)

    loads[0].wait()
    planes, rows, width = field.shape[2:]
    half = width // 2
    diagonal = lax.broadcasted_iota(jnp.int32, (rows, rows), 0) == lax.broadcasted_iota(jnp.int32, (rows, rows), 1)
    def moments_of_plane(z, carry):
        for b in range(2):
            lanes = slice(b * half, (b + 1) * half)
            across = jnp.broadcast_to(material_ref[z, b : b + 1, :].astype(F32), (rows, rows))
            which = jnp.sum(jnp.where(diagonal, across, 0.0), axis=1, keepdims=True)
            which = jnp.broadcast_to(which, (rows, half))
            masks = [which == float(m) for m in range(3)]

            def tensor(r, i, j):
                value = jnp.full((rows, half), alpha_ref[i, j, r, 3], F32)
                for m in range(3):
                    value = jnp.where(masks[m], alpha_ref[i, j, r, m], value)
                return value

            values = [[field[r, j, z, :, lanes].astype(F32) for j in range(3)] for r in range(2)]
            for i in range(3):
                real = jnp.zeros((rows, half), F32)
                imag = jnp.zeros((rows, half), F32)
                for j in range(3):
                    t_re, t_im = tensor(0, i, j), tensor(1, i, j)
                    real = real + t_re * values[0][j] - t_im * values[1][j]
                    imag = imag + t_re * values[1][j] + t_im * values[0][j]
                mom[i, z, :, b * half : (b + 1) * half] = real.astype(BF16)
                mom[i, z, :, width + b * half : width + (b + 1) * half] = imag.astype(BF16)
        return carry

    lax.fori_loop(0, planes, moments_of_plane, 0)

    def exchange(send, recv, ss, rs, index, axis):
        count, me = (n_zg, g) if axis == "zg" else (n_xy, q)

        def step_of(step, carry):
            if axis == "xy" and count == 32:
                x, y, z = lax.rem(q, 4), lax.rem(q // 4, 4), q // 16
                k = step - 1
                peer_x = lax.rem(x + far_first(lax.rem(k, 4)), 4)
                peer_y = lax.rem(y + far_first(lax.rem(k // 4, 4)), 4)
                peer_z = lax.rem(z + 1 - k // 16, 2)
                peer = peer_z * 16 + peer_y * 4 + peer_x
            else:
                peer = lax.rem(me + step, count)
            target = (peer, q) if axis == "zg" else (g, peer)
            pltpu.make_async_remote_copy(
                send.at[index, peer], recv.at[index, me], ss.at[index], rs.at[index],
                device_id=target, device_id_type=MESH,
            ).start()
            return carry

        lax.fori_loop(1, count, step_of, 0)
        recv[index, me] = send[index, me]

    def arrived(recv, rs, index):
        others = recv.at[index, pl.ds(0, recv.shape[1] - 1)]
        pltpu.make_async_copy(others, others, rs.at[index]).wait()

    loads[1].wait()
    spectrum = dot(mom[...].reshape(3 * planes * rows, 2 * width), ty[...]).astype(BF16)
    plane_rows = planes * rows
    lanes2 = spectrum.shape[1] // n_zg
    for i in range(3):
        for p in range(n_zg):
            a_send[i, p] = spectrum[i * plane_rows : (i + 1) * plane_rows, p * lanes2 : (p + 1) * lanes2]
    pl.semaphore_wait(barrier, n_xy + n_zg - 2)
    for i in range(3):
        exchange(a_send, a_recv, a_ss, a_rs, i, "zg")
    for load in loads[3:]:
        load.start()

    loads[2].wait()

    def forward_z(i, carry):
        arrived(a_recv, a_rs, i)
        operand = a_recv[i].reshape(n_zg * plane_rows, lanes2)
        b_send[i] = dot(tz[...], stacked(operand)).astype(BF16).reshape(b_send.shape[1:])
        exchange(b_send, b_recv, b_ss, b_rs, i, "xy")
        return carry

    lax.fori_loop(0, 3, forward_z, 0)

    block = lanes2 // 2
    length_x = prod.shape[0]
    step_rows = 128
    loads[4].wait()

    def weigh(step, carry):
        at = pl.ds(pl.multiple_of(step * step_rows, step_rows), step_rows)
        for c in range(6):
            for r in range(2):
                weighted[r, c, at, :] = green[r, c, at, :].astype(F32) * scale_ref[0, c]
        for i in range(3):
            total[i, at, :] = jnp.zeros((step_rows, lanes2), F32)
        return carry

    lax.fori_loop(0, length_x // step_rows, weigh, 0)

    loads[3].wait()
    loads[5].wait()
    rows_x = n_xy * rows

    def added(i, j, at):
        c = jnp.where(i == j, i, i + j + 2)
        spectrum = spec[at, :].astype(F32)
        s_re, s_im = spectrum[:, :block], spectrum[:, block:]
        g_re, g_im = weighted[0, c, at, :], weighted[1, c, at, :]
        real = total[i, at, :block] + g_re * s_re - g_im * s_im
        imag = total[i, at, block:] + g_re * s_im + g_im * s_re
        return real, imag

    def forward_x(j, carry):
        arrived(b_recv, b_rs, j)
        operand = b_recv[j].reshape(rows_x, lanes2)
        spec[...] = dot(tx[...], stacked(operand)).astype(BF16)

        def accumulate(step, carry):
            at = pl.ds(pl.multiple_of(step * step_rows, step_rows), step_rows)
            for i in range(3):
                real, imag = added(i, j, at)
                total[i, at, :block] = real
                total[i, at, block:] = imag
            return carry

        return lax.fori_loop(0, jnp.where(j < 2, length_x // step_rows, 0), accumulate, carry)

    lax.fori_loop(0, 3, forward_x, 0)

    def inverse_x(i, carry):
        def finish(step, carry):
            at = pl.ds(pl.multiple_of(step * step_rows, step_rows), step_rows)
            real, imag = added(i, 2, at)
            prod[at, :block] = real.astype(BF16)
            prod[at, block:] = imag.astype(BF16)
            return carry

        lax.fori_loop(0, length_x // step_rows, finish, 0)
        c_send[i] = dot(ux[...], stacked(prod[...])).astype(BF16).reshape(c_send.shape[1:])
        exchange(c_send, c_recv, c_ss, c_rs, i, "xy")
        return carry

    lax.fori_loop(0, 3, inverse_x, 0)

    loads[6].wait()

    def inverse_z(i, carry):
        arrived(c_recv, c_rs, i)
        operand = c_recv[i].reshape(rows_x, lanes2)
        d_send[i] = dot(uz[...], stacked(operand)).astype(BF16).reshape(d_send.shape[1:])
        exchange(d_send, d_recv, d_ss, d_rs, i, "zg")
        return carry

    lax.fori_loop(0, 3, inverse_z, 0)

    loads[7].wait()
    def inverse_y(i, carry):
        arrived(d_recv, d_rs, i)
        operand = jnp.concatenate([d_recv[i, p] for p in range(n_zg)], axis=1)
        back = dot(operand, uy[...])
        for r in range(2):
            part = back[:, r * width : (r + 1) * width].reshape(planes, rows, width)
            out[r, i] = (field[r, i].astype(F32) - part * norm).astype(BF16)
        return carry

    lax.fori_loop(0, 3, inverse_y, 0)

    for send, ss in ((a_send, a_ss), (b_send, b_ss), (c_send, c_ss), (d_send, d_ss)):
        for i in range(3):
            arrived(send, ss, i)


def hand_out(held_ref, out_hbm, sem):
    store = pltpu.make_async_copy(held_ref, out_hbm, sem)
    store.start()
    store.wait()


def on_device(dipole_field, material, alpha_table, green_spectrum, green_scale):
    n_zg = lax.axis_size("zg")
    n_xy = lax.axis_size("xy")
    _, _, planes, rows, width = dipole_field.shape
    planes_z, rows_x = planes * n_zg, rows * n_xy
    tables = tables_of(width, planes_z, rows_x, n_zg, n_xy)
    norm = 1.0 / float(8 * width * planes_z * rows_x)
    green = green_spectrum.reshape(green_spectrum.shape[:2] + green_spectrum.shape[3:])
    material = material.transpose(0, 2, 1)
    alpha_table = alpha_table.transpose(2, 3, 1, 0)
    green_scale = green_scale.transpose(1, 0)
    block = 2 * width // n_zg
    plane_rows = planes * rows
    dma = lambda n: pltpu.SemaphoreType.DMA((n,))
    over_zg = pltpu.VMEM((3, n_zg, plane_rows, 2 * block), BF16)
    over_xy = pltpu.VMEM((3, n_xy, rows, 2 * block), BF16)
    anywhere = pl.BlockSpec(memory_space=pl.ANY)
    vmem = pl.BlockSpec(memory_space=pltpu.VMEM)
    smem = pl.BlockSpec(memory_space=pltpu.SMEM)
    operands = [dipole_field, material, alpha_table, green, green_scale, *[jnp.asarray(t) for t in tables]]
    operands = [pltpu.with_memory_space_constraint(x, pltpu.HBM) for x in operands]
    held = pl.pallas_call(
        functools.partial(kernel, n_zg, n_xy, norm),
        out_shape=jax.ShapeDtypeStruct(dipole_field.shape, BF16),
        in_specs=[anywhere, vmem, smem, anywhere, smem] + [anywhere] * 6,
        out_specs=vmem,
        scratch_shapes=[
            pltpu.VMEM(dipole_field.shape, BF16),
            pltpu.VMEM(green.shape, BF16),
        ]
        + [pltpu.VMEM(t.shape, BF16) for t in tables]
        + [
            pltpu.VMEM((3, planes, rows, 2 * width), BF16),
            over_zg, over_zg, over_xy, over_xy,
            pltpu.VMEM((2 * rows_x, 2 * block), BF16),
            pltpu.VMEM(green.shape, F32),
            pltpu.VMEM((3, 2 * rows_x, 2 * block), F32),
            pltpu.VMEM((2 * rows_x, 2 * block), BF16),
            over_xy, over_xy, over_zg, over_zg,
            dma(8),
        ]
        + [dma(3)] * 8,
        compiler_params=pltpu.CompilerParams(
            collective_id=0, has_side_effects=True, vmem_limit_bytes=48 * 1024 * 1024
        ),
        cost_estimate=pl.CostEstimate(flops=5_000_000_000, bytes_accessed=12_000_000, transcendentals=0),
    )(*operands)
    return pl.pallas_call(
        hand_out,
        out_shape=jax.ShapeDtypeStruct(dipole_field.shape, BF16),
        in_specs=[vmem],
        out_specs=anywhere,
        scratch_shapes=[pltpu.SemaphoreType.DMA],
        compiler_params=pltpu.CompilerParams(vmem_limit_bytes=4 * 1024 * 1024),
    )(held)


def solution(mesh):
    return jax.shard_map(
        on_device,
        mesh=mesh,
        in_specs=(
            P(None, None, "zg", "xy", None),
            P("zg", "xy", None),
            P(),
            P(None, None, "xy", None, "zg"),
            P(None, "xy"),
        ),
        out_specs=P(None, None, "zg", "xy", None),
        check_vma=False,
    )
```

```python
import functools
import math

import jax
import jax.numpy as jnp
import ml_dtypes
import numpy as np
from jax import lax
from jax.experimental import pallas as pl
from jax.experimental.pallas import tpu as pltpu
from jax.sharding import PartitionSpec as P

MESH = pl.DeviceIdType.MESH
F32 = jnp.float32
BF16 = jnp.bfloat16

pairing = ((0, 3, 4), (3, 1, 5), (4, 5, 2))


def dft_table(count_in, count_out, length, direction):
    phases = (np.arange(count_in)[:, None] * np.arange(count_out)[None, :] % length).astype(np.float32)
    phases = phases * np.float32(2.0 * math.pi / length)
    cosine = np.cos(phases).astype(ml_dtypes.bfloat16).astype(np.float32)
    sine = (np.float32(direction) * np.sin(phases)).astype(ml_dtypes.bfloat16).astype(np.float32)
    return cosine, sine


def tables_of(rows_y, planes_z, rows_x, n_zg, n_xy):
    length_y, length_z, length_x = 2 * rows_y, 2 * planes_z, 2 * rows_x
    block_y = length_y // n_zg
    local_x = rows_x // n_xy
    eye = np.eye(local_x, dtype=np.float32)
    eye = np.concatenate([eye[0::2], eye[1::2]])
    c, s = dft_table(rows_y, length_y, length_y, -1.0)
    full = np.block([[c, s], [-s, c]]).reshape(2 * rows_y, 2, n_zg, block_y)
    forward_y = full.transpose(0, 2, 1, 3).reshape(2 * rows_y, 2 * length_y)
    c, s = dft_table(planes_z, length_z, length_z, -1.0)
    forward_z = np.concatenate([np.kron(c.T, eye), np.kron(s.T, eye)], axis=1)
    c, s = dft_table(rows_x, length_x, length_x, -1.0)
    c, s = c[:, :rows_x], s[:, :rows_x]
    forward_x = np.stack([np.concatenate([c[p::2].T, s[p::2].T], axis=1) for p in range(2)])
    c, s = dft_table(length_x, rows_x, length_x, 1.0)
    c, s = c[:rows_x], s[:rows_x]
    inverse_x = np.stack([np.concatenate([c[:, p::2].T, s[:, p::2].T], axis=1) for p in range(2)])
    c, s = dft_table(length_z, planes_z, length_z, 1.0)
    inverse_z = np.concatenate([np.kron(c.T, eye.T), np.kron(s.T, eye.T)], axis=1)
    c, s = dft_table(length_y, rows_y, length_y, 1.0)
    full = np.block([[c, s], [-s, c]]).reshape(2, n_zg, block_y, 2 * rows_y)
    inverse_y = full.transpose(1, 0, 2, 3).reshape(2 * length_y, 2 * rows_y)
    return [
        np.ascontiguousarray(t).astype(ml_dtypes.bfloat16)
        for t in (forward_y, forward_z, forward_x, inverse_x, inverse_z, inverse_y)
    ]


def times_i(pair):
    half = pair.shape[1] // 2
    return jnp.concatenate([-pair[:, half:], pair[:, :half]], axis=1)


def stacked(pair):
    return jnp.concatenate([pair, times_i(pair)], axis=0)


def far_first(d):
    return 2 + d + (d // 2) * (1 - 2 * d)


def dot(a, b):
    return jnp.dot(a, b, preferred_element_type=F32)


def kernel(
    n_zg, n_xy, norm,
    field_hbm, material_ref, alpha_ref, green_hbm, scale_ref,
    ty_hbm, tz_hbm, tx_hbm, ux_hbm, uz_hbm, uy_hbm,
    out,
    field, green, ty, tz, tx, ux, uz, uy,
    mom, a_send, a_recv, b_send, b_recv, spec, weighted, total, prod, c_send, c_recv, d_send, d_recv,
    load_sem, a_ss, a_rs, b_ss, b_rs, c_ss, c_rs, d_ss, d_rs,
):
    g = lax.axis_index("zg")
    q = lax.axis_index("xy")
    loads = [
        pltpu.make_async_copy(src, dst, load_sem.at[index])
        for index, (src, dst) in enumerate(
            (
                (field_hbm, field), (ty_hbm, ty), (tz_hbm, tz), (tx_hbm, tx),
                (green_hbm, green), (ux_hbm, ux), (uz_hbm, uz), (uy_hbm, uy),
            )
        )
    ]
    for load in loads[:3]:
        load.start()

    barrier = pltpu.get_barrier_semaphore()

    def greet_xy(step, carry):
        peer = lax.rem(q + step, n_xy)
        pl.semaphore_signal(barrier, inc=1, device_id=(g, peer), device_id_type=MESH)
        return carry

    def greet_zg(step, carry):
        peer = lax.rem(g + step, n_zg)
        pl.semaphore_signal(barrier, inc=1, device_id=(peer, q), device_id_type=MESH)
        return carry

    lax.fori_loop(1, n_xy, greet_xy, 0)
    lax.fori_loop(1, n_zg, greet_zg, 0)

    loads[0].wait()
    planes, rows, width = field.shape[2:]
    half = width // 2
    diagonal = lax.broadcasted_iota(jnp.int32, (rows, rows), 0) == lax.broadcasted_iota(jnp.int32, (rows, rows), 1)
    def moments_of_plane(z, carry):
        for b in range(2):
            lanes = slice(b * half, (b + 1) * half)
            across = jnp.broadcast_to(material_ref[z, b : b + 1, :].astype(F32), (rows, rows))
            which = jnp.sum(jnp.where(diagonal, across, 0.0), axis=1, keepdims=True)
            which = jnp.broadcast_to(which, (rows, half))
            masks = [which == float(m) for m in range(3)]

            def tensor(r, i, j):
                value = jnp.full((rows, half), alpha_ref[i, j, r, 3], F32)
                for m in range(3):
                    value = jnp.where(masks[m], alpha_ref[i, j, r, m], value)
                return value

            values = [[field[r, j, z, :, lanes].astype(F32) for j in range(3)] for r in range(2)]
            for i in range(3):
                real = jnp.zeros((rows, half), F32)
                imag = jnp.zeros((rows, half), F32)
                for j in range(3):
                    t_re, t_im = tensor(0, i, j), tensor(1, i, j)
                    real = real + t_re * values[0][j] - t_im * values[1][j]
                    imag = imag + t_re * values[1][j] + t_im * values[0][j]
                mom[i, z, :, b * half : (b + 1) * half] = real.astype(BF16)
                mom[i, z, :, width + b * half : width + (b + 1) * half] = imag.astype(BF16)
        return carry

    lax.fori_loop(0, planes, moments_of_plane, 0)

    def exchange(send, recv, ss, rs, index, axis):
        count, me = (n_zg, g) if axis == "zg" else (n_xy, q)

        def step_of(step, carry):
            if axis == "xy" and count == 32:
                x, y, z = lax.rem(q, 4), lax.rem(q // 4, 4), q // 16
                k = step - 1
                peer_x = lax.rem(x + far_first(lax.rem(k, 4)), 4)
                peer_y = lax.rem(y + far_first(lax.rem(k // 4, 4)), 4)
                peer_z = lax.rem(z + 1 - k // 16, 2)
                peer = peer_z * 16 + peer_y * 4 + peer_x
            else:
                peer = lax.rem(me + step, count)
            target = (peer, q) if axis == "zg" else (g, peer)
            pltpu.make_async_remote_copy(
                send.at[index, peer], recv.at[index, me], ss.at[index], rs.at[index],
                device_id=target, device_id_type=MESH,
            ).start()
            return carry

        lax.fori_loop(1, count, step_of, 0)
        recv[index, me] = send[index, me]

    def arrived(recv, rs, index):
        others = recv.at[index, pl.ds(0, recv.shape[1] - 1)]
        pltpu.make_async_copy(others, others, rs.at[index]).wait()

    loads[1].wait()
    spectrum = dot(mom[...].reshape(3 * planes * rows, 2 * width), ty[...]).astype(BF16)
    plane_rows = planes * rows
    lanes2 = spectrum.shape[1] // n_zg
    for i in range(3):
        for p in range(n_zg):
            a_send[i, p] = spectrum[i * plane_rows : (i + 1) * plane_rows, p * lanes2 : (p + 1) * lanes2]
    pl.semaphore_wait(barrier, n_xy + n_zg - 2)
    for i in range(3):
        exchange(a_send, a_recv, a_ss, a_rs, i, "zg")
    for load in loads[3:]:
        load.start()

    loads[2].wait()

    def forward_z(i, carry):
        arrived(a_recv, a_rs, i)
        operand = a_recv[i].reshape(n_zg * plane_rows, lanes2)
        b_send[i] = dot(tz[...], stacked(operand)).astype(BF16).reshape(b_send.shape[1:])
        exchange(b_send, b_recv, b_ss, b_rs, i, "xy")
        return carry

    lax.fori_loop(0, 3, forward_z, 0)

    block = lanes2 // 2
    half_x = prod.shape[1]
    length_x = 2 * half_x
    step_rows = 128
    finish_rows = 64
    loads[4].wait()

    def weigh(step, carry):
        at = pl.ds(pl.multiple_of(step * step_rows, step_rows), step_rows)
        for c in range(6):
            for r in range(2):
                weighted[r, c, at, :] = green[r, c, at, :].astype(F32) * scale_ref[0, c]
        for i in range(3):
            total[i, at, :] = jnp.zeros((step_rows, lanes2), F32)
        return carry

    lax.fori_loop(0, length_x // step_rows, weigh, 0)

    loads[3].wait()
    loads[5].wait()
    rows_x = n_xy * rows

    def added(i, j, at):
        c = jnp.where(i == j, i, i + j + 2)
        spectrum = spec[at, :].astype(F32)
        s_re, s_im = spectrum[:, :block], spectrum[:, block:]
        g_re, g_im = weighted[0, c, at, :], weighted[1, c, at, :]
        real = total[i, at, :block] + g_re * s_re - g_im * s_im
        imag = total[i, at, block:] + g_re * s_im + g_im * s_re
        return real, imag

    def forward_x(j, carry):
        arrived(b_recv, b_rs, j)
        wide = b_recv[j].astype(F32)
        even = wide[:, : rows // 2].reshape(half_x // 2, lanes2).astype(BF16)
        odd = wide[:, rows // 2 :].reshape(half_x // 2, lanes2).astype(BF16)
        even = dot(tx[0], stacked(even))
        odd = dot(tx[1], stacked(odd))
        spec[:half_x] = (even + odd).astype(BF16)
        spec[half_x:] = (even - odd).astype(BF16)

        def accumulate(step, carry):
            at = pl.ds(pl.multiple_of(step * step_rows, step_rows), step_rows)
            for i in range(3):
                real, imag = added(i, j, at)
                total[i, at, :block] = real
                total[i, at, block:] = imag
            return carry

        return lax.fori_loop(0, jnp.where(j < 2, length_x // step_rows, 0), accumulate, carry)

    lax.fori_loop(0, 3, forward_x, 0)

    def inverse_x(i, carry):
        def finish(step, carry):
            start = step * finish_rows
            at = pl.ds(pl.multiple_of(start, finish_rows), finish_rows)
            low = added(i, 2, at)
            high = added(i, 2, pl.ds(pl.multiple_of(start + half_x, finish_rows), finish_rows))
            for r in range(2):
                prod[0, at, r * block : (r + 1) * block] = (low[r] + high[r]).astype(BF16)
                prod[1, at, r * block : (r + 1) * block] = (low[r] - high[r]).astype(BF16)
            return carry

        lax.fori_loop(0, half_x // finish_rows, finish, 0)
        parts = [dot(ux[p], stacked(prod[p])).reshape(n_xy, rows // 2, lanes2) for p in range(2)]
        c_send[i] = jnp.concatenate(parts, axis=1).astype(BF16)
        exchange(c_send, c_recv, c_ss, c_rs, i, "xy")
        return carry

    lax.fori_loop(0, 3, inverse_x, 0)

    loads[6].wait()

    def inverse_z(i, carry):
        arrived(c_recv, c_rs, i)
        operand = c_recv[i].reshape(rows_x, lanes2)
        d_send[i] = dot(uz[...], stacked(operand)).astype(BF16).reshape(d_send.shape[1:])
        exchange(d_send, d_recv, d_ss, d_rs, i, "zg")
        return carry

    lax.fori_loop(0, 3, inverse_z, 0)

    loads[7].wait()
    def inverse_y(i, carry):
        arrived(d_recv, d_rs, i)
        operand = jnp.concatenate([d_recv[i, p] for p in range(n_zg)], axis=1)
        back = dot(operand, uy[...])
        for r in range(2):
            part = back[:, r * width : (r + 1) * width].reshape(planes, rows, width)
            out[r, i] = (field[r, i].astype(F32) - part * norm).astype(BF16)
        return carry

    lax.fori_loop(0, 3, inverse_y, 0)

    for send, ss in ((a_send, a_ss), (b_send, b_ss), (c_send, c_ss), (d_send, d_ss)):
        for i in range(3):
            arrived(send, ss, i)


def hand_out(held_ref, out_hbm, sem):
    store = pltpu.make_async_copy(held_ref, out_hbm, sem)
    store.start()
    store.wait()


def on_device(dipole_field, material, alpha_table, green_spectrum, green_scale):
    n_zg = lax.axis_size("zg")
    n_xy = lax.axis_size("xy")
    _, _, planes, rows, width = dipole_field.shape
    planes_z, rows_x = planes * n_zg, rows * n_xy
    tables = tables_of(width, planes_z, rows_x, n_zg, n_xy)
    norm = 1.0 / float(8 * width * planes_z * rows_x)
    green = green_spectrum.reshape(green_spectrum.shape[:2] + green_spectrum.shape[3:])
    material = material.transpose(0, 2, 1)
    alpha_table = alpha_table.transpose(2, 3, 1, 0)
    green_scale = green_scale.transpose(1, 0)
    block = 2 * width // n_zg
    plane_rows = planes * rows
    dma = lambda n: pltpu.SemaphoreType.DMA((n,))
    over_zg = pltpu.VMEM((3, n_zg, plane_rows, 2 * block), BF16)
    over_xy = pltpu.VMEM((3, n_xy, rows, 2 * block), BF16)
    anywhere = pl.BlockSpec(memory_space=pl.ANY)
    vmem = pl.BlockSpec(memory_space=pltpu.VMEM)
    smem = pl.BlockSpec(memory_space=pltpu.SMEM)
    operands = [dipole_field, material, alpha_table, green, green_scale, *[jnp.asarray(t) for t in tables]]
    operands = [pltpu.with_memory_space_constraint(x, pltpu.HBM) for x in operands]
    held = pl.pallas_call(
        functools.partial(kernel, n_zg, n_xy, norm),
        out_shape=jax.ShapeDtypeStruct(dipole_field.shape, BF16),
        in_specs=[anywhere, vmem, smem, anywhere, smem] + [anywhere] * 6,
        out_specs=vmem,
        scratch_shapes=[
            pltpu.VMEM(dipole_field.shape, BF16),
            pltpu.VMEM(green.shape, BF16),
        ]
        + [pltpu.VMEM(t.shape, BF16) for t in tables]
        + [
            pltpu.VMEM((3, planes, rows, 2 * width), BF16),
            over_zg, over_zg, over_xy, over_xy,
            pltpu.VMEM((2 * rows_x, 2 * block), BF16),
            pltpu.VMEM(green.shape, F32),
            pltpu.VMEM((3, 2 * rows_x, 2 * block), F32),
            pltpu.VMEM((2, rows_x, 2 * block), BF16),
            over_xy, over_xy, over_zg, over_zg,
            dma(8),
        ]
        + [dma(3)] * 8,
        compiler_params=pltpu.CompilerParams(
            collective_id=0, has_side_effects=True, vmem_limit_bytes=48 * 1024 * 1024
        ),
        cost_estimate=pl.CostEstimate(flops=5_000_000_000, bytes_accessed=12_000_000, transcendentals=0),
    )(*operands)
    return pl.pallas_call(
        hand_out,
        out_shape=jax.ShapeDtypeStruct(dipole_field.shape, BF16),
        in_specs=[vmem],
        out_specs=anywhere,
        scratch_shapes=[pltpu.SemaphoreType.DMA],
        compiler_params=pltpu.CompilerParams(vmem_limit_bytes=4 * 1024 * 1024),
    )(held)


def solution(mesh):
    return jax.shard_map(
        on_device,
        mesh=mesh,
        in_specs=(
            P(None, None, "zg", "xy", None),
            P("zg", "xy", None),
            P(),
            P(None, None, "xy", None, "zg"),
            P(None, "xy"),
        ),
        out_specs=P(None, None, "zg", "xy", None),
        check_vma=False,
    )
```

```python
import functools
import math

import jax
import jax.numpy as jnp
import ml_dtypes
import numpy as np
from jax import lax
from jax.experimental import pallas as pl
from jax.experimental.pallas import tpu as pltpu
from jax.sharding import PartitionSpec as P

MESH = pl.DeviceIdType.MESH
F32 = jnp.float32
BF16 = jnp.bfloat16

pairing = ((0, 3, 4), (3, 1, 5), (4, 5, 2))


def dft_table(count_in, count_out, length, direction):
    phases = (np.arange(count_in)[:, None] * np.arange(count_out)[None, :] % length).astype(np.float32)
    phases = phases * np.float32(2.0 * math.pi / length)
    cosine = np.cos(phases).astype(ml_dtypes.bfloat16).astype(np.float32)
    sine = (np.float32(direction) * np.sin(phases)).astype(ml_dtypes.bfloat16).astype(np.float32)
    return cosine, sine


def tables_of(rows_y, planes_z, rows_x, n_zg, n_xy):
    length_y, length_z, length_x = 2 * rows_y, 2 * planes_z, 2 * rows_x
    block_y = length_y // n_zg
    local_x = rows_x // n_xy
    eye = np.eye(local_x, dtype=np.float32)
    eye = np.concatenate([eye[0::2], eye[1::2]])
    c, s = dft_table(rows_y, length_y, length_y, -1.0)
    full = np.block([[c, s], [-s, c]]).reshape(2 * rows_y, 2, n_zg, block_y)
    forward_y = full.transpose(0, 2, 1, 3).reshape(2 * rows_y, 2 * length_y)
    c, s = dft_table(planes_z, length_z, length_z, -1.0)
    forward_z = np.concatenate([np.kron(c.T, eye), np.kron(s.T, eye)], axis=1)
    c, s = dft_table(rows_x, length_x, length_x, -1.0)
    c, s = c[:, :rows_x], s[:, :rows_x]
    forward_x = np.stack([np.concatenate([c[p::2].T, s[p::2].T], axis=1) for p in range(2)])
    c, s = dft_table(length_x, rows_x, length_x, 1.0)
    c, s = c[:rows_x], s[:rows_x]
    inverse_x = np.stack([np.concatenate([c[:, p::2].T, s[:, p::2].T], axis=1) for p in range(2)])
    c, s = dft_table(length_z, planes_z, length_z, 1.0)
    inverse_z = np.concatenate([np.kron(c.T, eye.T), np.kron(s.T, eye.T)], axis=1)
    c, s = dft_table(length_y, rows_y, length_y, 1.0)
    full = np.block([[c, s], [-s, c]]).reshape(2, n_zg, block_y, 2 * rows_y)
    inverse_y = full.transpose(1, 0, 2, 3).reshape(2 * length_y, 2 * rows_y)
    return [
        np.ascontiguousarray(t).astype(ml_dtypes.bfloat16)
        for t in (forward_y, forward_z, forward_x, inverse_x, inverse_z, inverse_y)
    ]


def times_i(pair):
    half = pair.shape[1] // 2
    return jnp.concatenate([-pair[:, half:], pair[:, :half]], axis=1)


def stacked(pair):
    return jnp.concatenate([pair, times_i(pair)], axis=0)


def far_first(d):
    return 2 + d + (d // 2) * (1 - 2 * d)


def dot(a, b):
    return jnp.dot(a, b, preferred_element_type=F32)


def kernel(
    n_zg, n_xy, norm,
    field_hbm, material_ref, alpha_ref, green_hbm, scale_ref,
    ty_hbm, tz_hbm, tx_hbm, ux_hbm, uz_hbm, uy_hbm,
    out,
    field, green, ty, tz, tx, ux, uz, uy,
    mom, a_send, a_recv, b_send, b_recv, spec, weighted, total, prod, c_send, c_recv, d_send, d_recv,
    load_sem, a_ss, a_rs, b_ss, b_rs, c_ss, c_rs, d_ss, d_rs, row_sem, plane_sem,
):
    g = lax.axis_index("zg")
    q = lax.axis_index("xy")
    loads = [
        pltpu.make_async_copy(src, dst, load_sem.at[index])
        for index, (src, dst) in enumerate(
            (
                (field_hbm, field), (ty_hbm, ty), (tz_hbm, tz), (tx_hbm, tx),
                (green_hbm, green), (ux_hbm, ux), (uz_hbm, uz), (uy_hbm, uy),
            )
        )
    ]
    for load in loads[:3]:
        load.start()

    barrier = pltpu.get_barrier_semaphore()

    x, y, zl = lax.rem(q, 4), lax.rem(q // 4, 4), q // 16
    peers_x = [(g, q - x + lax.rem(x + step, 4)) for step in (2, 1, 3)]
    peers_y = [(g, q + 4 * (lax.rem(y + step, 4) - y)) for step in (2, 1, 3)]
    peer_zl = (g, lax.rem(q + 16, 32))
    peers_zg = [(lax.rem(g + step, n_zg), q) for step in (2, 1, 3)]
    for peer in peers_zg + peers_x + peers_y + [peer_zl]:
        pl.semaphore_signal(barrier, inc=1, device_id=peer, device_id_type=MESH)

    loads[0].wait()
    planes, rows, width = field.shape[2:]
    half = width // 2
    diagonal = lax.broadcasted_iota(jnp.int32, (rows, rows), 0) == lax.broadcasted_iota(jnp.int32, (rows, rows), 1)
    def moments_of_plane(z, carry):
        for b in range(2):
            lanes = slice(b * half, (b + 1) * half)
            across = jnp.broadcast_to(material_ref[z, b : b + 1, :].astype(F32), (rows, rows))
            which = jnp.sum(jnp.where(diagonal, across, 0.0), axis=1, keepdims=True)
            which = jnp.broadcast_to(which, (rows, half))
            masks = [which == float(m) for m in range(3)]

            def tensor(r, i, j):
                value = jnp.full((rows, half), alpha_ref[i, j, r, 3], F32)
                for m in range(3):
                    value = jnp.where(masks[m], alpha_ref[i, j, r, m], value)
                return value

            values = [[field[r, j, z, :, lanes].astype(F32) for j in range(3)] for r in range(2)]
            for i in range(3):
                real = jnp.zeros((rows, half), F32)
                imag = jnp.zeros((rows, half), F32)
                for j in range(3):
                    t_re, t_im = tensor(0, i, j), tensor(1, i, j)
                    real = real + t_re * values[0][j] - t_im * values[1][j]
                    imag = imag + t_re * values[1][j] + t_im * values[0][j]
                mom[i, z, :, b * half : (b + 1) * half] = real.astype(BF16)
                mom[i, z, :, width + b * half : width + (b + 1) * half] = imag.astype(BF16)
        return carry

    lax.fori_loop(0, planes, moments_of_plane, 0)

    def exchange(send, recv, ss, rs, index, axis):
        count, me = (n_zg, g) if axis == "zg" else (n_xy, q)

        def step_of(step, carry):
            if axis == "xy" and count == 32:
                x, y, z = lax.rem(q, 4), lax.rem(q // 4, 4), q // 16
                k = step - 1
                peer_x = lax.rem(x + far_first(lax.rem(k, 4)), 4)
                peer_y = lax.rem(y + far_first(lax.rem(k // 4, 4)), 4)
                peer_z = lax.rem(z + 1 - k // 16, 2)
                peer = peer_z * 16 + peer_y * 4 + peer_x
            else:
                peer = lax.rem(me + step, count)
            target = (peer, q) if axis == "zg" else (g, peer)
            pltpu.make_async_remote_copy(
                send.at[index, peer], recv.at[index, me], ss.at[index], rs.at[index],
                device_id=target, device_id_type=MESH,
            ).start()
            return carry

        lax.fori_loop(1, count, step_of, 0)
        recv[index, me] = send[index, me]

    def arrived(recv, rs, index):
        others = recv.at[index, pl.ds(0, recv.shape[1] - 1)]
        pltpu.make_async_copy(others, others, rs.at[index]).wait()

    loads[1].wait()
    spectrum = dot(mom[...].reshape(3 * planes * rows, 2 * width), ty[...]).astype(BF16)
    plane_rows = planes * rows
    lanes2 = spectrum.shape[1] // n_zg
    for i in range(3):
        for p in range(n_zg):
            a_send[i, p] = spectrum[i * plane_rows : (i + 1) * plane_rows, p * lanes2 : (p + 1) * lanes2]
    pl.semaphore_wait(barrier, 10)
    for peer in peers_y:
        pl.semaphore_signal(row_sem, inc=1, device_id=peer, device_id_type=MESH)
    for i in range(3):
        exchange(a_send, a_recv, a_ss, a_rs, i, "zg")
    for load in loads[3:]:
        load.start()

    pl.semaphore_wait(row_sem, 3)
    pl.semaphore_signal(plane_sem, inc=1, device_id=peer_zl, device_id_type=MESH)

    loads[2].wait()

    def forward_z(i, carry):
        arrived(a_recv, a_rs, i)
        operand = a_recv[i].reshape(n_zg * plane_rows, lanes2)
        b_send[i] = dot(tz[...], stacked(operand)).astype(BF16).reshape(b_send.shape[1:])

        @pl.when(i == 0)
        def _():
            pl.semaphore_wait(plane_sem, 1)

        exchange(b_send, b_recv, b_ss, b_rs, i, "xy")
        return carry

    lax.fori_loop(0, 3, forward_z, 0)

    block = lanes2 // 2
    half_x = prod.shape[1]
    length_x = 2 * half_x
    step_rows = 128
    finish_rows = 64
    loads[4].wait()

    def weigh(step, carry):
        at = pl.ds(pl.multiple_of(step * step_rows, step_rows), step_rows)
        for c in range(6):
            for r in range(2):
                weighted[r, c, at, :] = green[r, c, at, :].astype(F32) * scale_ref[0, c]
        for i in range(3):
            total[i, at, :] = jnp.zeros((step_rows, lanes2), F32)
        return carry

    lax.fori_loop(0, length_x // step_rows, weigh, 0)

    loads[3].wait()
    loads[5].wait()
    rows_x = n_xy * rows

    def added(i, j, at):
        c = jnp.where(i == j, i, i + j + 2)
        spectrum = spec[at, :].astype(F32)
        s_re, s_im = spectrum[:, :block], spectrum[:, block:]
        g_re, g_im = weighted[0, c, at, :], weighted[1, c, at, :]
        real = total[i, at, :block] + g_re * s_re - g_im * s_im
        imag = total[i, at, block:] + g_re * s_im + g_im * s_re
        return real, imag

    def forward_x(j, carry):
        arrived(b_recv, b_rs, j)
        wide = b_recv[j].astype(F32)
        even = wide[:, : rows // 2].reshape(half_x // 2, lanes2).astype(BF16)
        odd = wide[:, rows // 2 :].reshape(half_x // 2, lanes2).astype(BF16)
        even = dot(tx[0], stacked(even))
        odd = dot(tx[1], stacked(odd))
        spec[:half_x] = (even + odd).astype(BF16)
        spec[half_x:] = (even - odd).astype(BF16)

        def accumulate(step, carry):
            at = pl.ds(pl.multiple_of(step * step_rows, step_rows), step_rows)
            for i in range(3):
                real, imag = added(i, j, at)
                total[i, at, :block] = real
                total[i, at, block:] = imag
            return carry

        return lax.fori_loop(0, jnp.where(j < 2, length_x // step_rows, 0), accumulate, carry)

    lax.fori_loop(0, 3, forward_x, 0)

    def inverse_x(i, carry):
        def finish(step, carry):
            start = step * finish_rows
            at = pl.ds(pl.multiple_of(start, finish_rows), finish_rows)
            low = added(i, 2, at)
            high = added(i, 2, pl.ds(pl.multiple_of(start + half_x, finish_rows), finish_rows))
            for r in range(2):
                prod[0, at, r * block : (r + 1) * block] = (low[r] + high[r]).astype(BF16)
                prod[1, at, r * block : (r + 1) * block] = (low[r] - high[r]).astype(BF16)
            return carry

        lax.fori_loop(0, half_x // finish_rows, finish, 0)
        parts = [dot(ux[p], stacked(prod[p])).reshape(n_xy, rows // 2, lanes2) for p in range(2)]
        c_send[i] = jnp.concatenate(parts, axis=1).astype(BF16)
        exchange(c_send, c_recv, c_ss, c_rs, i, "xy")
        return carry

    lax.fori_loop(0, 3, inverse_x, 0)

    loads[6].wait()

    def inverse_z(i, carry):
        arrived(c_recv, c_rs, i)
        operand = c_recv[i].reshape(rows_x, lanes2)
        d_send[i] = dot(uz[...], stacked(operand)).astype(BF16).reshape(d_send.shape[1:])
        exchange(d_send, d_recv, d_ss, d_rs, i, "zg")
        return carry

    lax.fori_loop(0, 3, inverse_z, 0)

    loads[7].wait()
    def inverse_y(i, carry):
        arrived(d_recv, d_rs, i)
        operand = jnp.concatenate([d_recv[i, p] for p in range(n_zg)], axis=1)
        back = dot(operand, uy[...])
        for r in range(2):
            part = back[:, r * width : (r + 1) * width].reshape(planes, rows, width)
            out[r, i] = (field[r, i].astype(F32) - part * norm).astype(BF16)
        return carry

    lax.fori_loop(0, 3, inverse_y, 0)

    for send, ss in ((a_send, a_ss), (b_send, b_ss), (c_send, c_ss), (d_send, d_ss)):
        for i in range(3):
            arrived(send, ss, i)


def hand_out(held_ref, out_hbm, sem):
    store = pltpu.make_async_copy(held_ref, out_hbm, sem)
    store.start()
    store.wait()


def on_device(dipole_field, material, alpha_table, green_spectrum, green_scale):
    n_zg = lax.axis_size("zg")
    n_xy = lax.axis_size("xy")
    _, _, planes, rows, width = dipole_field.shape
    planes_z, rows_x = planes * n_zg, rows * n_xy
    tables = tables_of(width, planes_z, rows_x, n_zg, n_xy)
    norm = 1.0 / float(8 * width * planes_z * rows_x)
    green = green_spectrum.reshape(green_spectrum.shape[:2] + green_spectrum.shape[3:])
    material = material.transpose(0, 2, 1)
    alpha_table = alpha_table.transpose(2, 3, 1, 0)
    green_scale = green_scale.transpose(1, 0)
    block = 2 * width // n_zg
    plane_rows = planes * rows
    dma = lambda n: pltpu.SemaphoreType.DMA((n,))
    over_zg = pltpu.VMEM((3, n_zg, plane_rows, 2 * block), BF16)
    over_xy = pltpu.VMEM((3, n_xy, rows, 2 * block), BF16)
    anywhere = pl.BlockSpec(memory_space=pl.ANY)
    vmem = pl.BlockSpec(memory_space=pltpu.VMEM)
    smem = pl.BlockSpec(memory_space=pltpu.SMEM)
    operands = [dipole_field, material, alpha_table, green, green_scale, *[jnp.asarray(t) for t in tables]]
    operands = [pltpu.with_memory_space_constraint(x, pltpu.HBM) for x in operands]
    held = pl.pallas_call(
        functools.partial(kernel, n_zg, n_xy, norm),
        out_shape=jax.ShapeDtypeStruct(dipole_field.shape, BF16),
        in_specs=[anywhere, vmem, smem, anywhere, smem] + [anywhere] * 6,
        out_specs=vmem,
        scratch_shapes=[
            pltpu.VMEM(dipole_field.shape, BF16),
            pltpu.VMEM(green.shape, BF16),
        ]
        + [pltpu.VMEM(t.shape, BF16) for t in tables]
        + [
            pltpu.VMEM((3, planes, rows, 2 * width), BF16),
            over_zg, over_zg, over_xy, over_xy,
            pltpu.VMEM((2 * rows_x, 2 * block), BF16),
            pltpu.VMEM(green.shape, F32),
            pltpu.VMEM((3, 2 * rows_x, 2 * block), F32),
            pltpu.VMEM((2, rows_x, 2 * block), BF16),
            over_xy, over_xy, over_zg, over_zg,
            dma(8),
        ]
        + [dma(3)] * 8
        + [pltpu.SemaphoreType.REGULAR] * 2,
        compiler_params=pltpu.CompilerParams(
            collective_id=0, has_side_effects=True, vmem_limit_bytes=48 * 1024 * 1024
        ),
        cost_estimate=pl.CostEstimate(flops=5_000_000_000, bytes_accessed=12_000_000, transcendentals=0),
    )(*operands)
    return pl.pallas_call(
        hand_out,
        out_shape=jax.ShapeDtypeStruct(dipole_field.shape, BF16),
        in_specs=[vmem],
        out_specs=anywhere,
        scratch_shapes=[pltpu.SemaphoreType.DMA],
        compiler_params=pltpu.CompilerParams(vmem_limit_bytes=4 * 1024 * 1024),
    )(held)


def solution(mesh):
    return jax.shard_map(
        on_device,
        mesh=mesh,
        in_specs=(
            P(None, None, "zg", "xy", None),
            P("zg", "xy", None),
            P(),
            P(None, None, "xy", None, "zg"),
            P(None, "xy"),
        ),
        out_specs=P(None, None, "zg", "xy", None),
        check_vma=False,
    )
```

```python
import functools
import math

import jax
import jax.numpy as jnp
import ml_dtypes
import numpy as np
from jax import lax
from jax.experimental import pallas as pl
from jax.experimental.pallas import tpu as pltpu
from jax.sharding import PartitionSpec as P

MESH = pl.DeviceIdType.MESH
F32 = jnp.float32
BF16 = jnp.bfloat16

xy_steps = sorted(
    [(zl, y, x) for zl in range(2) for y in range(4) for x in range(4) if (zl, y, x) != (0, 0, 0)],
    key=lambda s: (-s[0], -min(s[1], 4 - s[1]) - min(s[2], 4 - s[2])),
)


def dft_table(count_in, count_out, length, direction):
    phases = (np.arange(count_in)[:, None] * np.arange(count_out)[None, :] % length).astype(np.float32)
    phases = phases * np.float32(2.0 * math.pi / length)
    cosine = np.cos(phases).astype(ml_dtypes.bfloat16).astype(np.float32)
    sine = (np.float32(direction) * np.sin(phases)).astype(ml_dtypes.bfloat16).astype(np.float32)
    return cosine, sine


def tables_of(rows_y, planes_z, rows_x, n_zg, n_xy):
    length_y, length_z, length_x = 2 * rows_y, 2 * planes_z, 2 * rows_x
    block_y = length_y // n_zg
    local_x = rows_x // n_xy
    eye = np.eye(local_x, dtype=np.float32)
    eye = np.concatenate([eye[0::2], eye[1::2]])
    c, s = dft_table(rows_y, length_y, length_y, -1.0)
    full = np.block([[c, s], [-s, c]]).reshape(2 * rows_y, 2, n_zg, block_y)
    forward_y = full.transpose(0, 2, 1, 3).reshape(2 * rows_y, 2 * length_y)
    c, s = dft_table(planes_z, length_z, length_z, -1.0)
    forward_z = np.concatenate([np.kron(c.T, eye), np.kron(s.T, eye)], axis=1)
    c, s = dft_table(rows_x, length_x, length_x, -1.0)
    c, s = c[:, :rows_x], s[:, :rows_x]
    forward_x = np.stack([np.concatenate([c[p::2].T, s[p::2].T], axis=1) for p in range(2)])
    c, s = dft_table(length_x, rows_x, length_x, 1.0)
    c, s = c[:rows_x], s[:rows_x]
    inverse_x = np.stack([np.concatenate([c[:, p::2].T, s[:, p::2].T], axis=1) for p in range(2)])
    c, s = dft_table(length_z, planes_z, length_z, 1.0)
    inverse_z = np.concatenate([np.kron(c.T, eye.T), np.kron(s.T, eye.T)], axis=1)
    c, s = dft_table(length_y, rows_y, length_y, 1.0)
    full = np.block([[c, s], [-s, c]]).reshape(2, n_zg, block_y, 2 * rows_y)
    inverse_y = full.transpose(1, 0, 2, 3).reshape(2 * length_y, 2 * rows_y)
    return [
        np.ascontiguousarray(t).astype(ml_dtypes.bfloat16)
        for t in (forward_y, forward_z, forward_x, inverse_x, inverse_z, inverse_y)
    ]


def times_i(pair):
    half = pair.shape[1] // 2
    return jnp.concatenate([-pair[:, half:], pair[:, :half]], axis=1)


def stacked(pair):
    return jnp.concatenate([pair, times_i(pair)], axis=0)


def far_first(d):
    return 2 + d + (d // 2) * (1 - 2 * d)


def dot(a, b):
    return jnp.dot(a, b, preferred_element_type=F32)


def kernel(
    n_zg, n_xy, norm,
    field_hbm, material_ref, alpha_ref, green_hbm, scale_ref,
    ty_hbm, tz_hbm, tx_hbm, ux_hbm, uz_hbm, uy_hbm,
    out,
    field, green, ty, tz, tx, ux, uz, uy,
    mom, a_send, a_recv, b_send, b_recv, spec, weighted, total, prod, c_send, c_recv, d_send, d_recv,
    load_sem, a_ss, a_rs, b_ss, b_rs, c_ss, c_rs, d_ss, d_rs, row_sem, plane_sem,
):
    g = lax.axis_index("zg")
    q = lax.axis_index("xy")
    loads = [
        pltpu.make_async_copy(src, dst, load_sem.at[index])
        for index, (src, dst) in enumerate(
            (
                (field_hbm, field), (ty_hbm, ty), (tz_hbm, tz), (tx_hbm, tx),
                (green_hbm, green), (ux_hbm, ux), (uz_hbm, uz), (uy_hbm, uy),
            )
        )
    ]
    for load in loads[:3]:
        load.start()

    barrier = pltpu.get_barrier_semaphore()

    x, y, zl = lax.rem(q, 4), lax.rem(q // 4, 4), q // 16
    peers_x = [(g, q - x + lax.rem(x + step, 4)) for step in (2, 1, 3)]
    peers_y = [(g, q + 4 * (lax.rem(y + step, 4) - y)) for step in (2, 1, 3)]
    peer_zl = (g, lax.rem(q + 16, 32))
    peers_zg = [(lax.rem(g + step, n_zg), q) for step in (2, 1, 3)]
    for peer in peers_zg + peers_x + peers_y + [peer_zl]:
        pl.semaphore_signal(barrier, inc=1, device_id=peer, device_id_type=MESH)

    loads[0].wait()
    planes, rows, width = field.shape[2:]
    half = width // 2
    diagonal = lax.broadcasted_iota(jnp.int32, (rows, rows), 0) == lax.broadcasted_iota(jnp.int32, (rows, rows), 1)
    def moments_of_plane(z, carry):
        for b in range(2):
            lanes = slice(b * half, (b + 1) * half)
            across = jnp.broadcast_to(material_ref[z, b : b + 1, :].astype(F32), (rows, rows))
            which = jnp.sum(jnp.where(diagonal, across, 0.0), axis=1, keepdims=True)
            which = jnp.broadcast_to(which, (rows, half))
            masks = [which == float(m) for m in range(3)]

            def tensor(r, i, j):
                value = jnp.full((rows, half), alpha_ref[i, j, r, 3], F32)
                for m in range(3):
                    value = jnp.where(masks[m], alpha_ref[i, j, r, m], value)
                return value

            values = [[field[r, j, z, :, lanes].astype(F32) for j in range(3)] for r in range(2)]
            for i in range(3):
                real = jnp.zeros((rows, half), F32)
                imag = jnp.zeros((rows, half), F32)
                for j in range(3):
                    t_re, t_im = tensor(0, i, j), tensor(1, i, j)
                    real = real + t_re * values[0][j] - t_im * values[1][j]
                    imag = imag + t_re * values[1][j] + t_im * values[0][j]
                mom[i, z, :, b * half : (b + 1) * half] = real.astype(BF16)
                mom[i, z, :, width + b * half : width + (b + 1) * half] = imag.astype(BF16)
        return carry

    lax.fori_loop(0, planes, moments_of_plane, 0)

    def exchange(send, recv, ss, rs, index, axis):
        count, me = (n_zg, g) if axis == "zg" else (n_xy, q)

        def step_of(step, carry):
            if axis == "xy" and count == 32:
                x, y, z = lax.rem(q, 4), lax.rem(q // 4, 4), q // 16
                k = step - 1
                peer_x = lax.rem(x + far_first(lax.rem(k, 4)), 4)
                peer_y = lax.rem(y + far_first(lax.rem(k // 4, 4)), 4)
                peer_z = lax.rem(z + 1 - k // 16, 2)
                peer = peer_z * 16 + peer_y * 4 + peer_x
            else:
                peer = lax.rem(me + step, count)
            target = (peer, q) if axis == "zg" else (g, peer)
            pltpu.make_async_remote_copy(
                send.at[index, peer], recv.at[index, me], ss.at[index], rs.at[index],
                device_id=target, device_id_type=MESH,
            ).start()
            return carry

        lax.fori_loop(1, count, step_of, 0)
        recv[index, me] = send[index, me]

    at_x = [lax.rem(x + step, 4) for step in range(4)]
    at_y = [lax.rem(y + step, 4) * 4 for step in range(4)]
    at_zl = [zl * 16, lax.rem(zl + 1, 2) * 16]

    def exchange_xy(send, recv, ss, rs, index):
        for s_zl, s_y, s_x in xy_steps:
            peer = at_zl[s_zl] + at_y[s_y] + at_x[s_x]
            pltpu.make_async_remote_copy(
                send.at[index, peer], recv.at[index, q], ss.at[index], rs.at[index],
                device_id=(g, peer), device_id_type=MESH,
            ).start()
        recv[index, q] = send[index, q]

    def arrived(recv, rs, index):
        others = recv.at[index, pl.ds(0, recv.shape[1] - 1)]
        pltpu.make_async_copy(others, others, rs.at[index]).wait()

    loads[1].wait()
    plane_rows = planes * rows
    lanes2 = ty.shape[1] // n_zg

    def forward_y(i, carry):
        spectrum = dot(mom[i].reshape(plane_rows, 2 * width), ty[...]).astype(BF16)
        for p in range(n_zg):
            a_send[i, p] = spectrum[:, p * lanes2 : (p + 1) * lanes2]

        @pl.when(i == 0)
        def _():
            pl.semaphore_wait(barrier, 10)
            for peer in peers_y:
                pl.semaphore_signal(row_sem, inc=1, device_id=peer, device_id_type=MESH)

        exchange(a_send, a_recv, a_ss, a_rs, i, "zg")
        return carry

    lax.fori_loop(0, 3, forward_y, 0)
    for load in loads[3:]:
        load.start()

    pl.semaphore_wait(row_sem, 3)
    pl.semaphore_signal(plane_sem, inc=1, device_id=peer_zl, device_id_type=MESH)

    loads[2].wait()

    def forward_z(i, carry):
        arrived(a_recv, a_rs, i)
        operand = a_recv[i].reshape(n_zg * plane_rows, lanes2)
        b_send[i] = dot(tz[...], stacked(operand)).astype(BF16).reshape(b_send.shape[1:])

        @pl.when(i == 0)
        def _():
            pl.semaphore_wait(plane_sem, 1)

        exchange_xy(b_send, b_recv, b_ss, b_rs, i)
        return carry

    lax.fori_loop(0, 3, forward_z, 0)

    block = lanes2 // 2
    half_x = prod.shape[1]
    length_x = 2 * half_x
    step_rows = 128
    finish_rows = 64
    loads[4].wait()

    def weigh(step, carry):
        at = pl.ds(pl.multiple_of(step * step_rows, step_rows), step_rows)
        for c in range(6):
            for r in range(2):
                weighted[r, c, at, :] = green[r, c, at, :].astype(F32) * scale_ref[0, c]
        for i in range(3):
            total[i, at, :] = jnp.zeros((step_rows, lanes2), F32)
        return carry

    lax.fori_loop(0, length_x // step_rows, weigh, 0)

    loads[3].wait()
    loads[5].wait()
    rows_x = n_xy * rows

    def added(i, j, at):
        c = jnp.where(i == j, i, i + j + 2)
        spectrum = spec[at, :].astype(F32)
        s_re, s_im = spectrum[:, :block], spectrum[:, block:]
        g_re, g_im = weighted[0, c, at, :], weighted[1, c, at, :]
        real = total[i, at, :block] + g_re * s_re - g_im * s_im
        imag = total[i, at, block:] + g_re * s_im + g_im * s_re
        return real, imag

    def forward_x(j, carry):
        arrived(b_recv, b_rs, j)
        wide = b_recv[j].astype(F32)
        even = wide[:, : rows // 2].reshape(half_x // 2, lanes2).astype(BF16)
        odd = wide[:, rows // 2 :].reshape(half_x // 2, lanes2).astype(BF16)
        even = dot(tx[0], stacked(even))
        odd = dot(tx[1], stacked(odd))
        spec[:half_x] = (even + odd).astype(BF16)
        spec[half_x:] = (even - odd).astype(BF16)

        def accumulate(step, carry):
            at = pl.ds(pl.multiple_of(step * step_rows, step_rows), step_rows)
            for i in range(3):
                real, imag = added(i, j, at)
                total[i, at, :block] = real
                total[i, at, block:] = imag
            return carry

        return lax.fori_loop(0, jnp.where(j < 2, length_x // step_rows, 0), accumulate, carry)

    lax.fori_loop(0, 3, forward_x, 0)

    def inverse_x(i, carry):
        def finish(step, carry):
            start = step * finish_rows
            at = pl.ds(pl.multiple_of(start, finish_rows), finish_rows)
            low = added(i, 2, at)
            high = added(i, 2, pl.ds(pl.multiple_of(start + half_x, finish_rows), finish_rows))
            for r in range(2):
                prod[0, at, r * block : (r + 1) * block] = (low[r] + high[r]).astype(BF16)
                prod[1, at, r * block : (r + 1) * block] = (low[r] - high[r]).astype(BF16)
            return carry

        lax.fori_loop(0, half_x // finish_rows, finish, 0)
        parts = [dot(ux[p], stacked(prod[p])).reshape(n_xy, rows // 2, lanes2) for p in range(2)]
        c_send[i] = jnp.concatenate(parts, axis=1).astype(BF16)
        exchange_xy(c_send, c_recv, c_ss, c_rs, i)
        return carry

    lax.fori_loop(0, 3, inverse_x, 0)

    loads[6].wait()

    def inverse_z(i, carry):
        arrived(c_recv, c_rs, i)
        operand = c_recv[i].reshape(rows_x, lanes2)
        d_send[i] = dot(uz[...], stacked(operand)).astype(BF16).reshape(d_send.shape[1:])
        exchange(d_send, d_recv, d_ss, d_rs, i, "zg")
        return carry

    lax.fori_loop(0, 3, inverse_z, 0)

    loads[7].wait()
    def inverse_y(i, carry):
        arrived(d_recv, d_rs, i)
        operand = jnp.concatenate([d_recv[i, p] for p in range(n_zg)], axis=1)
        back = dot(operand, uy[...])
        for r in range(2):
            part = back[:, r * width : (r + 1) * width].reshape(planes, rows, width)
            out[r, i] = (field[r, i].astype(F32) - part * norm).astype(BF16)
        return carry

    lax.fori_loop(0, 3, inverse_y, 0)

    for send, ss in ((a_send, a_ss), (b_send, b_ss), (c_send, c_ss), (d_send, d_ss)):
        for i in range(3):
            arrived(send, ss, i)


def hand_out(held_ref, out_hbm, sem):
    store = pltpu.make_async_copy(held_ref, out_hbm, sem)
    store.start()
    store.wait()


def on_device(dipole_field, material, alpha_table, green_spectrum, green_scale):
    n_zg = lax.axis_size("zg")
    n_xy = lax.axis_size("xy")
    _, _, planes, rows, width = dipole_field.shape
    planes_z, rows_x = planes * n_zg, rows * n_xy
    tables = tables_of(width, planes_z, rows_x, n_zg, n_xy)
    norm = 1.0 / float(8 * width * planes_z * rows_x)
    green = green_spectrum.reshape(green_spectrum.shape[:2] + green_spectrum.shape[3:])
    material = material.transpose(0, 2, 1)
    alpha_table = alpha_table.transpose(2, 3, 1, 0)
    green_scale = green_scale.transpose(1, 0)
    block = 2 * width // n_zg
    plane_rows = planes * rows
    dma = lambda n: pltpu.SemaphoreType.DMA((n,))
    over_zg = pltpu.VMEM((3, n_zg, plane_rows, 2 * block), BF16)
    over_xy = pltpu.VMEM((3, n_xy, rows, 2 * block), BF16)
    anywhere = pl.BlockSpec(memory_space=pl.ANY)
    vmem = pl.BlockSpec(memory_space=pltpu.VMEM)
    smem = pl.BlockSpec(memory_space=pltpu.SMEM)
    operands = [dipole_field, material, alpha_table, green, green_scale, *[jnp.asarray(t) for t in tables]]
    operands = [pltpu.with_memory_space_constraint(x, pltpu.HBM) for x in operands]
    held = pl.pallas_call(
        functools.partial(kernel, n_zg, n_xy, norm),
        out_shape=jax.ShapeDtypeStruct(dipole_field.shape, BF16),
        in_specs=[anywhere, vmem, smem, anywhere, smem] + [anywhere] * 6,
        out_specs=vmem,
        scratch_shapes=[
            pltpu.VMEM(dipole_field.shape, BF16),
            pltpu.VMEM(green.shape, BF16),
        ]
        + [pltpu.VMEM(t.shape, BF16) for t in tables]
        + [
            pltpu.VMEM((3, planes, rows, 2 * width), BF16),
            over_zg, over_zg, over_xy, over_xy,
            pltpu.VMEM((2 * rows_x, 2 * block), BF16),
            pltpu.VMEM(green.shape, F32),
            pltpu.VMEM((3, 2 * rows_x, 2 * block), F32),
            pltpu.VMEM((2, rows_x, 2 * block), BF16),
            over_xy, over_xy, over_zg, over_zg,
            dma(8),
        ]
        + [dma(3)] * 8
        + [pltpu.SemaphoreType.REGULAR] * 2,
        compiler_params=pltpu.CompilerParams(
            collective_id=0, has_side_effects=True, vmem_limit_bytes=48 * 1024 * 1024
        ),
        cost_estimate=pl.CostEstimate(flops=5_000_000_000, bytes_accessed=12_000_000, transcendentals=0),
    )(*operands)
    return pl.pallas_call(
        hand_out,
        out_shape=jax.ShapeDtypeStruct(dipole_field.shape, BF16),
        in_specs=[vmem],
        out_specs=anywhere,
        scratch_shapes=[pltpu.SemaphoreType.DMA],
        compiler_params=pltpu.CompilerParams(vmem_limit_bytes=4 * 1024 * 1024),
    )(held)


def solution(mesh):
    return jax.shard_map(
        on_device,
        mesh=mesh,
        in_specs=(
            P(None, None, "zg", "xy", None),
            P("zg", "xy", None),
            P(),
            P(None, None, "xy", None, "zg"),
            P(None, "xy"),
        ),
        out_specs=P(None, None, "zg", "xy", None),
        check_vma=False,
    )
```

```python
import functools
import math

import jax
import jax.numpy as jnp
import ml_dtypes
import numpy as np
from jax import lax
from jax.experimental import pallas as pl
from jax.experimental.pallas import tpu as pltpu
from jax.sharding import PartitionSpec as P

MESH = pl.DeviceIdType.MESH
F32 = jnp.float32
BF16 = jnp.bfloat16

xy_steps = sorted(
    [(zl, y, x) for zl in range(2) for y in range(4) for x in range(4) if (zl, y, x) != (0, 0, 0)],
    key=lambda s: (-s[0], -min(s[1], 4 - s[1]) - min(s[2], 4 - s[2])),
)


def dft_table(count_in, count_out, length, direction):
    phases = (np.arange(count_in)[:, None] * np.arange(count_out)[None, :] % length).astype(np.float32)
    phases = phases * np.float32(2.0 * math.pi / length)
    cosine = np.cos(phases).astype(ml_dtypes.bfloat16).astype(np.float32)
    sine = (np.float32(direction) * np.sin(phases)).astype(ml_dtypes.bfloat16).astype(np.float32)
    return cosine, sine


def tables_of(rows_y, planes_z, rows_x, n_zg, n_xy):
    length_y, length_z, length_x = 2 * rows_y, 2 * planes_z, 2 * rows_x
    block_y = length_y // n_zg
    local_x = rows_x // n_xy
    eye = np.eye(local_x, dtype=np.float32)
    eye = np.concatenate([eye[0::2], eye[1::2]])
    c, s = dft_table(rows_y, length_y, length_y, -1.0)
    full = np.block([[c, s], [-s, c]]).reshape(2 * rows_y, 2, n_zg, block_y)
    forward_y = full.transpose(0, 2, 1, 3).reshape(2 * rows_y, 2 * length_y)
    c, s = dft_table(planes_z, length_z, length_z, -1.0)
    forward_z = np.concatenate([np.kron(c.T, eye), np.kron(s.T, eye)], axis=1)
    c, s = dft_table(rows_x, length_x, length_x, -1.0)
    c, s = c[:, :rows_x], s[:, :rows_x]
    forward_x = np.stack([np.concatenate([c[p::2].T, s[p::2].T], axis=1) for p in range(2)])
    c, s = dft_table(length_x, rows_x, length_x, 1.0)
    c, s = c[:rows_x], s[:rows_x]
    inverse_x = np.stack([np.concatenate([c[:, p::2].T, s[:, p::2].T], axis=1) for p in range(2)])
    c, s = dft_table(length_z, planes_z, length_z, 1.0)
    inverse_z = np.concatenate([np.kron(c.T, eye.T), np.kron(s.T, eye.T)], axis=1)
    c, s = dft_table(length_y, rows_y, length_y, 1.0)
    full = np.block([[c, s], [-s, c]]).reshape(2, n_zg, block_y, 2 * rows_y)
    inverse_y = full.transpose(1, 0, 2, 3).reshape(2 * length_y, 2 * rows_y)
    return [
        np.ascontiguousarray(t).astype(ml_dtypes.bfloat16)
        for t in (forward_y, forward_z, forward_x, inverse_x, inverse_z, inverse_y)
    ]


def times_i(pair):
    half = pair.shape[1] // 2
    return jnp.concatenate([-pair[:, half:], pair[:, :half]], axis=1)


def stacked(pair):
    return jnp.concatenate([pair, times_i(pair)], axis=0)


def far_first(d):
    return 2 + d + (d // 2) * (1 - 2 * d)


def dot(a, b):
    return jnp.dot(a, b, preferred_element_type=F32)


def kernel(
    n_zg, n_xy, norm,
    field_hbm, material_ref, alpha_ref, green_hbm, scale_ref,
    ty_hbm, tz_hbm, tx_hbm, ux_hbm, uz_hbm, uy_hbm,
    out,
    field, green, ty, tz, tx, ux, uz, uy,
    mom, a_send, a_recv, b_send, b_recv, spec, weighted, total, prod, c_send, c_recv, d_send, d_recv,
    load_sem, a_ss, a_rs, b_ss, b_rs, c_ss, c_rs, d_ss, d_rs, row_sem, plane_sem,
):
    g = lax.axis_index("zg")
    q = lax.axis_index("xy")
    loads = [
        pltpu.make_async_copy(src, dst, load_sem.at[index])
        for index, (src, dst) in enumerate(
            (
                (field_hbm, field), (ty_hbm, ty), (tz_hbm, tz), (tx_hbm, tx),
                (green_hbm, green), (ux_hbm, ux), (uz_hbm, uz), (uy_hbm, uy),
            )
        )
    ]
    for load in loads[:3]:
        load.start()

    barrier = pltpu.get_barrier_semaphore()

    x, y, zl = lax.rem(q, 4), lax.rem(q // 4, 4), q // 16
    peers_x = [(g, q - x + lax.rem(x + step, 4)) for step in (2, 1, 3)]
    peers_y = [(g, q + 4 * (lax.rem(y + step, 4) - y)) for step in (2, 1, 3)]
    peer_zl = (g, lax.rem(q + 16, 32))
    peers_zg = [(lax.rem(g + step, n_zg), q) for step in (2, 1, 3)]
    for peer in peers_zg + peers_x + peers_y + [peer_zl]:
        pl.semaphore_signal(barrier, inc=1, device_id=peer, device_id_type=MESH)

    loads[0].wait()
    planes, rows, width = field.shape[2:]
    half = width // 2
    diagonal = lax.broadcasted_iota(jnp.int32, (rows, rows), 0) == lax.broadcasted_iota(jnp.int32, (rows, rows), 1)
    def moments_of_plane(z, carry):
        for b in range(2):
            lanes = slice(b * half, (b + 1) * half)
            across = jnp.broadcast_to(material_ref[z, b : b + 1, :].astype(F32), (rows, rows))
            which = jnp.sum(jnp.where(diagonal, across, 0.0), axis=1, keepdims=True)
            which = jnp.broadcast_to(which, (rows, half))
            masks = [which == float(m) for m in range(3)]

            def tensor(r, i, j):
                value = jnp.full((rows, half), alpha_ref[i, j, r, 3], F32)
                for m in range(3):
                    value = jnp.where(masks[m], alpha_ref[i, j, r, m], value)
                return value

            values = [[field[r, j, z, :, lanes].astype(F32) for j in range(3)] for r in range(2)]
            for i in range(3):
                real = jnp.zeros((rows, half), F32)
                imag = jnp.zeros((rows, half), F32)
                for j in range(3):
                    t_re, t_im = tensor(0, i, j), tensor(1, i, j)
                    real = real + t_re * values[0][j] - t_im * values[1][j]
                    imag = imag + t_re * values[1][j] + t_im * values[0][j]
                mom[i, z, :, b * half : (b + 1) * half] = real.astype(BF16)
                mom[i, z, :, width + b * half : width + (b + 1) * half] = imag.astype(BF16)
        return carry

    lax.fori_loop(0, planes, moments_of_plane, 0)

    def exchange(send, recv, ss, rs, index, axis):
        count, me = (n_zg, g) if axis == "zg" else (n_xy, q)

        def step_of(step, carry):
            if axis == "xy" and count == 32:
                x, y, z = lax.rem(q, 4), lax.rem(q // 4, 4), q // 16
                k = step - 1
                peer_x = lax.rem(x + far_first(lax.rem(k, 4)), 4)
                peer_y = lax.rem(y + far_first(lax.rem(k // 4, 4)), 4)
                peer_z = lax.rem(z + 1 - k // 16, 2)
                peer = peer_z * 16 + peer_y * 4 + peer_x
            else:
                peer = lax.rem(me + step, count)
            target = (peer, q) if axis == "zg" else (g, peer)
            pltpu.make_async_remote_copy(
                send.at[index, peer], recv.at[index, me], ss.at[index], rs.at[index],
                device_id=target, device_id_type=MESH,
            ).start()
            return carry

        for step in range(1, count):
            step_of(step, 0)
        recv[index, me] = send[index, me]

    at_x = [lax.rem(x + step, 4) for step in range(4)]
    at_y = [lax.rem(y + step, 4) * 4 for step in range(4)]
    at_zl = [zl * 16, lax.rem(zl + 1, 2) * 16]

    def exchange_xy(send, recv, ss, rs, index):
        for s_zl, s_y, s_x in xy_steps:
            peer = at_zl[s_zl] + at_y[s_y] + at_x[s_x]
            pltpu.make_async_remote_copy(
                send.at[index, peer], recv.at[index, q], ss.at[index], rs.at[index],
                device_id=(g, peer), device_id_type=MESH,
            ).start()
        recv[index, q] = send[index, q]

    def arrived(recv, rs, index):
        others = recv.at[index, pl.ds(0, recv.shape[1] - 1)]
        pltpu.make_async_copy(others, others, rs.at[index]).wait()

    loads[1].wait()
    plane_rows = planes * rows
    lanes2 = ty.shape[1] // n_zg

    def forward_y(i, carry):
        spectrum = dot(mom[i].reshape(plane_rows, 2 * width), ty[...]).astype(BF16)
        for p in range(n_zg):
            a_send[i, p] = spectrum[:, p * lanes2 : (p + 1) * lanes2]

        @pl.when(i == 0)
        def _():
            pl.semaphore_wait(barrier, 10)
            for peer in peers_y:
                pl.semaphore_signal(row_sem, inc=1, device_id=peer, device_id_type=MESH)

        exchange(a_send, a_recv, a_ss, a_rs, i, "zg")
        return carry

    lax.fori_loop(0, 3, forward_y, 0)
    for load in loads[3:]:
        load.start()

    pl.semaphore_wait(row_sem, 3)
    pl.semaphore_signal(plane_sem, inc=1, device_id=peer_zl, device_id_type=MESH)

    loads[2].wait()

    def forward_z(i, carry):
        arrived(a_recv, a_rs, i)
        operand = a_recv[i].reshape(n_zg * plane_rows, lanes2)
        b_send[i] = dot(tz[...], stacked(operand)).astype(BF16).reshape(b_send.shape[1:])

        @pl.when(i == 0)
        def _():
            pl.semaphore_wait(plane_sem, 1)

        exchange_xy(b_send, b_recv, b_ss, b_rs, i)
        return carry

    lax.fori_loop(0, 3, forward_z, 0)

    block = lanes2 // 2
    half_x = prod.shape[1]
    length_x = 2 * half_x
    step_rows = 128
    finish_rows = 64
    loads[4].wait()

    def weigh(step, carry):
        at = pl.ds(pl.multiple_of(step * step_rows, step_rows), step_rows)
        for c in range(6):
            for r in range(2):
                weighted[r, c, at, :] = green[r, c, at, :].astype(F32) * scale_ref[0, c]
        for i in range(3):
            total[i, at, :] = jnp.zeros((step_rows, lanes2), F32)
        return carry

    lax.fori_loop(0, length_x // step_rows, weigh, 0)

    loads[3].wait()
    loads[5].wait()
    rows_x = n_xy * rows

    def added(i, j, at):
        c = jnp.where(i == j, i, i + j + 2)
        spectrum = spec[at, :].astype(F32)
        s_re, s_im = spectrum[:, :block], spectrum[:, block:]
        g_re, g_im = weighted[0, c, at, :], weighted[1, c, at, :]
        real = total[i, at, :block] + g_re * s_re - g_im * s_im
        imag = total[i, at, block:] + g_re * s_im + g_im * s_re
        return real, imag

    def forward_x(j, carry):
        arrived(b_recv, b_rs, j)
        wide = b_recv[j].astype(F32)
        even = wide[:, : rows // 2].reshape(half_x // 2, lanes2).astype(BF16)
        odd = wide[:, rows // 2 :].reshape(half_x // 2, lanes2).astype(BF16)
        even = dot(tx[0], stacked(even))
        odd = dot(tx[1], stacked(odd))
        spec[:half_x] = (even + odd).astype(BF16)
        spec[half_x:] = (even - odd).astype(BF16)

        def accumulate(step, carry):
            at = pl.ds(pl.multiple_of(step * step_rows, step_rows), step_rows)
            for i in range(3):
                real, imag = added(i, j, at)
                total[i, at, :block] = real
                total[i, at, block:] = imag
            return carry

        return lax.fori_loop(0, jnp.where(j < 2, length_x // step_rows, 0), accumulate, carry)

    lax.fori_loop(0, 3, forward_x, 0)

    def inverse_x(i, carry):
        def finish(step, carry):
            start = step * finish_rows
            at = pl.ds(pl.multiple_of(start, finish_rows), finish_rows)
            low = added(i, 2, at)
            high = added(i, 2, pl.ds(pl.multiple_of(start + half_x, finish_rows), finish_rows))
            for r in range(2):
                prod[0, at, r * block : (r + 1) * block] = (low[r] + high[r]).astype(BF16)
                prod[1, at, r * block : (r + 1) * block] = (low[r] - high[r]).astype(BF16)
            return carry

        lax.fori_loop(0, half_x // finish_rows, finish, 0)
        parts = [dot(ux[p], stacked(prod[p])).reshape(n_xy, rows // 2, lanes2) for p in range(2)]
        c_send[i] = jnp.concatenate(parts, axis=1).astype(BF16)
        exchange_xy(c_send, c_recv, c_ss, c_rs, i)
        return carry

    lax.fori_loop(0, 3, inverse_x, 0)

    loads[6].wait()

    def inverse_z(i, carry):
        arrived(c_recv, c_rs, i)
        operand = c_recv[i].reshape(rows_x, lanes2)
        d_send[i] = dot(uz[...], stacked(operand)).astype(BF16).reshape(d_send.shape[1:])
        exchange(d_send, d_recv, d_ss, d_rs, i, "zg")
        return carry

    lax.fori_loop(0, 3, inverse_z, 0)

    loads[7].wait()
    def inverse_y(i, carry):
        arrived(d_recv, d_rs, i)
        operand = jnp.concatenate([d_recv[i, p] for p in range(n_zg)], axis=1)
        back = dot(operand, uy[...])
        for r in range(2):
            part = back[:, r * width : (r + 1) * width].reshape(planes, rows, width)
            out[r, i] = (field[r, i].astype(F32) - part * norm).astype(BF16)
        return carry

    lax.fori_loop(0, 3, inverse_y, 0)

    for send, ss in ((a_send, a_ss), (b_send, b_ss), (c_send, c_ss), (d_send, d_ss)):
        for i in range(3):
            arrived(send, ss, i)


def hand_out(held_ref, out_hbm, sem):
    store = pltpu.make_async_copy(held_ref, out_hbm, sem)
    store.start()
    store.wait()


def on_device(dipole_field, material, alpha_table, green_spectrum, green_scale):
    n_zg = lax.axis_size("zg")
    n_xy = lax.axis_size("xy")
    _, _, planes, rows, width = dipole_field.shape
    planes_z, rows_x = planes * n_zg, rows * n_xy
    tables = tables_of(width, planes_z, rows_x, n_zg, n_xy)
    norm = 1.0 / float(8 * width * planes_z * rows_x)
    green = green_spectrum.reshape(green_spectrum.shape[:2] + green_spectrum.shape[3:])
    material = material.transpose(0, 2, 1)
    alpha_table = alpha_table.transpose(2, 3, 1, 0)
    green_scale = green_scale.transpose(1, 0)
    block = 2 * width // n_zg
    plane_rows = planes * rows
    dma = lambda n: pltpu.SemaphoreType.DMA((n,))
    over_zg = pltpu.VMEM((3, n_zg, plane_rows, 2 * block), BF16)
    over_xy = pltpu.VMEM((3, n_xy, rows, 2 * block), BF16)
    anywhere = pl.BlockSpec(memory_space=pl.ANY)
    vmem = pl.BlockSpec(memory_space=pltpu.VMEM)
    smem = pl.BlockSpec(memory_space=pltpu.SMEM)
    operands = [dipole_field, material, alpha_table, green, green_scale, *[jnp.asarray(t) for t in tables]]
    operands = [pltpu.with_memory_space_constraint(x, pltpu.HBM) for x in operands]
    held = pl.pallas_call(
        functools.partial(kernel, n_zg, n_xy, norm),
        out_shape=jax.ShapeDtypeStruct(dipole_field.shape, BF16),
        in_specs=[anywhere, vmem, smem, anywhere, smem] + [anywhere] * 6,
        out_specs=vmem,
        scratch_shapes=[
            pltpu.VMEM(dipole_field.shape, BF16),
            pltpu.VMEM(green.shape, BF16),
        ]
        + [pltpu.VMEM(t.shape, BF16) for t in tables]
        + [
            pltpu.VMEM((3, planes, rows, 2 * width), BF16),
            over_zg, over_zg, over_xy, over_xy,
            pltpu.VMEM((2 * rows_x, 2 * block), BF16),
            pltpu.VMEM(green.shape, F32),
            pltpu.VMEM((3, 2 * rows_x, 2 * block), F32),
            pltpu.VMEM((2, rows_x, 2 * block), BF16),
            over_xy, over_xy, over_zg, over_zg,
            dma(8),
        ]
        + [dma(3)] * 8
        + [pltpu.SemaphoreType.REGULAR] * 2,
        compiler_params=pltpu.CompilerParams(
            collective_id=0, has_side_effects=True, vmem_limit_bytes=48 * 1024 * 1024
        ),
        cost_estimate=pl.CostEstimate(flops=5_000_000_000, bytes_accessed=12_000_000, transcendentals=0),
    )(*operands)
    return pl.pallas_call(
        hand_out,
        out_shape=jax.ShapeDtypeStruct(dipole_field.shape, BF16),
        in_specs=[vmem],
        out_specs=anywhere,
        scratch_shapes=[pltpu.SemaphoreType.DMA],
        compiler_params=pltpu.CompilerParams(vmem_limit_bytes=4 * 1024 * 1024),
    )(held)


def solution(mesh):
    return jax.shard_map(
        on_device,
        mesh=mesh,
        in_specs=(
            P(None, None, "zg", "xy", None),
            P("zg", "xy", None),
            P(),
            P(None, None, "xy", None, "zg"),
            P(None, "xy"),
        ),
        out_specs=P(None, None, "zg", "xy", None),
        check_vma=False,
    )
```
